32 devices in a mesh: ma: 8 (over z, x), row: 4 (over y, core).
Axes of the slice: x: 2, y: 2, z: 4, core: 2. Of those that a mesh axis runs over, the one named last changes fastest.
Arguments:
- grid_field: bfloat16 [64, 1536, 512], P(None, 'ma', 'row'), may hold values from -6 to 6
- legendre: bfloat16 [64, 1024, 1536], P(('ma', 'row')), may hold values from -0.15625 to 0.15625
- order_table: int32 [64], P(('ma', 'row')), may hold values from 0 to 1023, as said below
- boundary_rows: int32 [2, 2], replicated, may hold values from 96 to 127, as said below
- inverse: bfloat16 [1024, 256, 256], P(('ma', 'row')), may hold values from -0.375 to 0.375
Outputs:
- spectra: bfloat16 [1024, 256, 128], P(('ma', 'row'))
The draws below stay inside these ranges and needn't reach their ends.
Inputs may be any that keep to these rules, and one draw needn't show every extreme that they name: `order_table`: slots 2 i and 2 i + 1 hold the orders m and 1023 - m of one pair, m < 512 first; no order appears twice; the pair of 0 and 1023 is always present. `boundary_rows`: the four entries differ and lie in the top 128 // 4 Chebyshev rows; both ends of that range occur.
All inputs are finite; a program needn't handle non-finite values.
Results may differ from the reference program's by a relative error of at most 0.0049.
Values may be sent and summed in bfloat16 or wider, within the bound.
A program may use at most 192 MiB of HBM per device.

```python
import jax
import jax.numpy as jnp
from jax import lax

L = 1024
NTHETA = 1536
NR = 128
M_WIN = 64


def draw_order_table(key, part):
    pair_count = M_WIN // 2
    first_key, second_key = jax.random.split(jax.random.fold_in(key, 11))
    others = jax.random.permutation(first_key, L // 2 - 1)[:pair_count - 1].astype(jnp.int32) + 1
    chosen = jnp.concatenate([jnp.zeros((1,), jnp.int32), others])
    chosen = jax.random.permutation(second_key, chosen).astype(jnp.int32)
    matched_pairs = jnp.stack([chosen, L - 1 - chosen], axis=1)
    return matched_pairs.reshape(M_WIN).astype(jnp.int32)


def draw_boundary_rows(key, part):
    quarter = NR // 4
    first_key, second_key = jax.random.split(jax.random.fold_in(key, 23))
    middle = jax.random.permutation(first_key, quarter - 2)[:2].astype(jnp.int32) + (NR - quarter + 1)
    ends = jnp.stack([jnp.full((), NR - 1, jnp.int32), jnp.full((), NR - quarter, jnp.int32)])
    values = jnp.concatenate([ends, middle])
    values = jax.random.permutation(second_key, values).astype(jnp.int32)
    return values.reshape(2, 2)


def block_scale(own_key, extent, cuts, low, largest):
    def one(position, shards_of):
        steps = jax.random.uniform(jax.random.fold_in(jax.random.fold_in(own_key, 6), position), (shards_of,), jnp.float32, low / len(cuts), largest / len(cuts))
        return jnp.repeat(jnp.exp(steps), extent[position] // shards_of).reshape((-1,) + (1,) * (len(extent) - position - 1))

    loudness = one(*cuts[0])
    for cut in cuts[1:]:
        loudness = loudness * one(*cut)
    return loudness


def centred(own_key, extent, spread, most, cuts=(), kind=jnp.bfloat16):
    entries = spread * jax.random.normal(own_key, extent, jnp.float32)
    if cuts:
        entries = entries * block_scale(own_key, extent, cuts, -0.22, 0.18)
    return jnp.clip(entries, -most, most).astype(kind)


def setup_inputs(seed: int = 0) -> dict:
    arg_keys = jax.random.split(jax.random.key(seed), 6)
    grid_field = centred(arg_keys[0], (M_WIN, NTHETA, 4 * NR), 1.0, 6.0, ((1, 8), (2, 4)))
    legendre = centred(arg_keys[1], (M_WIN, L, NTHETA), NTHETA ** -0.5, 0.15625, ((0, 32),))
    order_table = draw_order_table(jax.random.fold_in(arg_keys[5], 71), 0)
    boundary_rows = draw_boundary_rows(jax.random.fold_in(arg_keys[5], 71), 0)
    inverse = centred(arg_keys[4], (L, 2 * NR, 2 * NR), (2 * NR) ** -0.5, 0.375, ((0, 32),))
    return {"grid_field": grid_field, "legendre": legendre, "order_table": order_table, "boundary_rows": boundary_rows, "inverse": inverse}


def chebyshev_table(radial_levels):
    wave_number = jnp.arange(radial_levels, dtype=jnp.float32)[:, None]
    grid_point = jnp.arange(radial_levels, dtype=jnp.float32)[None, :]
    cos_table = jnp.cos(jnp.pi * wave_number * (grid_point + 0.5) / radial_levels) * jnp.sqrt(2.0 / radial_levels)
    return jnp.where(wave_number == 0.0, cos_table * jnp.sqrt(0.5), cos_table)

def boundary_keep(boundary_rows, radial_levels):
    row_index = jnp.arange(radial_levels, dtype=jnp.int32)[None, :]
    boundary_hit = (row_index == boundary_rows[:, 0:1]) | (row_index == boundary_rows[:, 1:2])
    return jnp.where(boundary_hit, 0.0, 1.0).astype(jnp.float32)

def reference(grid_field, legendre, order_table, boundary_rows, inverse):
    degrees = jnp.arange(L, dtype=jnp.int32)

    def one_slot(slot_items):
        table_rows, field_cols, order_value = slot_items
        matrix_product = jnp.dot(table_rows, field_cols, preferred_element_type=jnp.float32)
        return jnp.where((degrees >= order_value)[:, None], matrix_product, jnp.zeros_like(matrix_product))
    spectral_coefficients = lax.map(one_slot, (legendre, grid_field, order_table))
    spectral_coefficients = spectral_coefficients.reshape(M_WIN, L, NR, 2, 2)
    chebyshev = chebyshev_table(NR)
    coefficients = jnp.einsum('kj,sljqp->lqksp', chebyshev, spectral_coefficients, precision=lax.Precision.HIGHEST)
    keep_rows = boundary_keep(boundary_rows, NR)
    right_side = (coefficients * keep_rows[None, :, :, None, None]).reshape(L, 2 * NR, 2 * M_WIN)
    right_side = right_side.astype(jnp.bfloat16)

    def one_degree(degree_items):
        inverse_rows, right_rows = degree_items
        return jnp.dot(inverse_rows, right_rows, preferred_element_type=jnp.float32).astype(jnp.bfloat16)
    return lax.map(one_degree, (inverse, right_side))
```

```python
import jax
import jax.numpy as jnp
from jax import lax
from jax.sharding import PartitionSpec as P


def chebyshev_table(radial_levels):
    wave_number = jnp.arange(radial_levels, dtype=jnp.float32)[:, None]
    grid_point = jnp.arange(radial_levels, dtype=jnp.float32)[None, :]
    cos_table = jnp.cos(jnp.pi * wave_number * (grid_point + 0.5) / radial_levels) * jnp.sqrt(
        2.0 / radial_levels
    )
    return jnp.where(wave_number == 0.0, cos_table * jnp.sqrt(0.5), cos_table)


def boundary_keep(boundary_rows, radial_levels):
    row_index = jnp.arange(radial_levels, dtype=jnp.int32)[None, :]
    boundary_hit = (row_index == boundary_rows[:, 0:1]) | (row_index == boundary_rows[:, 1:2])
    return jnp.where(boundary_hit, 0.0, 1.0).astype(jnp.float32)


def radial_matrix(boundary_rows, radial_levels):
    cheb = chebyshev_table(radial_levels)
    keep = boundary_keep(boundary_rows, radial_levels)
    eye = jnp.eye(2, dtype=jnp.float32)
    full = (
        cheb.T[:, None, None, None, None, :]
        * eye[None, :, None, None, :, None]
        * eye[None, None, :, :, None, None]
        * keep[None, None, None, None, :, :]
    )
    return full.reshape(4 * radial_levels, 4 * radial_levels)


def on_device(grid_field, legendre, order_table, boundary_rows, inverse):
    ma_count = lax.axis_size("ma")
    row_count = lax.axis_size("row")
    devices = ma_count * row_count
    slots, degree_total, latitudes = legendre.shape
    columns = grid_field.shape[2]
    radial_levels = columns * row_count // 4
    share = degree_total // devices
    got = lax.all_to_all(
        grid_field.reshape(devices, slots, latitudes // ma_count, columns),
        ("ma", "row"), split_axis=0, concat_axis=0, tiled=True,
    )
    got = got.reshape(ma_count, row_count, slots, latitudes // ma_count, columns)
    got = got.transpose(2, 0, 3, 1, 4).reshape(slots, latitudes, row_count * columns)
    spectrum = jnp.einsum("xlt,xtd->xld", legendre, got, preferred_element_type=jnp.float32)
    degrees = jnp.arange(degree_total, dtype=jnp.int32)
    lower = degrees[None, :] >= order_table[:, None]
    spectrum = jnp.where(lower[:, :, None], spectrum, 0.0)
    matrix = radial_matrix(boundary_rows, radial_levels)
    matrix_high = matrix.astype(jnp.bfloat16)
    matrix_low = (matrix - matrix_high.astype(jnp.float32)).astype(jnp.bfloat16)
    high = spectrum.astype(jnp.bfloat16)
    low = (spectrum - high.astype(jnp.float32)).astype(jnp.bfloat16)

    def mul(a, b):
        return jnp.einsum("xld,de->xle", a, b, preferred_element_type=jnp.float32)

    right = mul(high, matrix_high) + (mul(low, matrix_high) + mul(high, matrix_low))
    right = right.astype(jnp.bfloat16).reshape(slots, degree_total, 2, 2 * radial_levels)
    right = right.transpose(1, 0, 2, 3).reshape(devices, share, 2 * slots, 2 * radial_levels)
    right = lax.all_to_all(right, ("ma", "row"), split_axis=0, concat_axis=0, tiled=True)
    right = right.transpose(1, 0, 2, 3).reshape(share, devices * 2 * slots, 2 * radial_levels)
    solved = jnp.einsum("lij,lnj->lin", inverse, right, preferred_element_type=jnp.float32)
    return solved.astype(jnp.bfloat16)


def solution(mesh):
    return jax.shard_map(
        on_device,
        mesh=mesh,
        in_specs=(
            P(None, "ma", "row"),
            P(("ma", "row"), None, None),
            P(("ma", "row")),
            P(),
            P(("ma", "row"), None, None),
        ),
        out_specs=P(("ma", "row"), None, None),
        check_vma=False,
    )
```

```python
import functools

import jax
import jax.numpy as jnp
import numpy as np
from jax import lax
from jax.experimental import pallas as pl
from jax.experimental.pallas import tpu as pltpu
from jax.sharding import PartitionSpec as P

MESH = pl.DeviceIdType.MESH
GROUP = 8
GROUPS = 4


def chebyshev_table(radial_levels):
    wave_number = jnp.arange(radial_levels, dtype=jnp.float32)[:, None]
    grid_point = jnp.arange(radial_levels, dtype=jnp.float32)[None, :]
    cos_table = jnp.cos(jnp.pi * wave_number * (grid_point + 0.5) / radial_levels) * jnp.sqrt(
        2.0 / radial_levels
    )
    return jnp.where(wave_number == 0.0, cos_table * jnp.sqrt(0.5), cos_table)


def boundary_keep(boundary_rows, radial_levels):
    row_index = jnp.arange(radial_levels, dtype=jnp.int32)[None, :]
    boundary_hit = (row_index == boundary_rows[:, 0:1]) | (row_index == boundary_rows[:, 1:2])
    return jnp.where(boundary_hit, 0.0, 1.0).astype(jnp.float32)


def radial_matrix(boundary_rows, radial_levels):
    cheb = chebyshev_table(radial_levels)
    keep = boundary_keep(boundary_rows, radial_levels)
    eye = jnp.eye(2, dtype=jnp.float32)
    full = (
        cheb.T[:, None, None, None, None, :]
        * eye[None, :, None, None, :, None]
        * eye[None, None, :, :, None, None]
        * keep[None, None, None, None, :, :]
    )
    return full.reshape(4 * radial_levels, 4 * radial_levels)


def with_collectives(grid_field, legendre, order_table, boundary_rows, inverse):
    ma_count = lax.axis_size("ma")
    row_count = lax.axis_size("row")
    devices = ma_count * row_count
    slots, degree_total, latitudes = legendre.shape
    columns = grid_field.shape[2]
    radial_levels = columns * row_count // 4
    share = degree_total // devices
    got = lax.all_to_all(
        grid_field.reshape(devices, slots, latitudes // ma_count, columns),
        ("ma", "row"), split_axis=0, concat_axis=0, tiled=True,
    )
    got = got.reshape(ma_count, row_count, slots, latitudes // ma_count, columns)
    got = got.transpose(2, 0, 3, 1, 4).reshape(slots, latitudes, row_count * columns)
    spectrum = jnp.einsum("xlt,xtd->xld", legendre, got, preferred_element_type=jnp.float32)
    degrees = jnp.arange(degree_total, dtype=jnp.int32)
    lower = degrees[None, :] >= order_table[:, None]
    spectrum = jnp.where(lower[:, :, None], spectrum, 0.0)
    matrix = radial_matrix(boundary_rows, radial_levels)
    matrix_high = matrix.astype(jnp.bfloat16)
    matrix_low = (matrix - matrix_high.astype(jnp.float32)).astype(jnp.bfloat16)
    high = spectrum.astype(jnp.bfloat16)
    low = (spectrum - high.astype(jnp.float32)).astype(jnp.bfloat16)

    def mul(a, b):
        return jnp.einsum("xld,de->xle", a, b, preferred_element_type=jnp.float32)

    right = mul(high, matrix_high) + (mul(low, matrix_high) + mul(high, matrix_low))
    right = right.astype(jnp.bfloat16).reshape(slots, degree_total, 2, 2 * radial_levels)
    right = right.transpose(1, 0, 2, 3).reshape(devices, share, 2 * slots, 2 * radial_levels)
    right = lax.all_to_all(right, ("ma", "row"), split_axis=0, concat_axis=0, tiled=True)
    right = right.transpose(1, 0, 2, 3).reshape(share, devices * 2 * slots, 2 * radial_levels)
    solved = jnp.einsum("lij,lnj->lin", inverse, right, preferred_element_type=jnp.float32)
    return solved.astype(jnp.bfloat16)


def radial_parts(radial_levels):
    wave_number = np.arange(radial_levels, dtype=np.float64)[:, None]
    point = np.arange(radial_levels, dtype=np.float64)[None, :] + 0.5
    cheb = np.cos(np.pi * wave_number * point / radial_levels) * np.sqrt(2.0 / radial_levels)
    cheb[0] *= np.sqrt(0.5)
    full = np.zeros((radial_levels, 2, 2, 2, 2, radial_levels), np.float32)
    for q in range(2):
        for p in range(2):
            full[:, q, p, p, q, :] = cheb.T
    full = full.reshape(4 * radial_levels, 4 * radial_levels)
    high = full.astype(jnp.bfloat16)
    low = (full - high.astype(np.float32)).astype(jnp.bfloat16)
    return np.stack([high, low])


def kernel(
    rows, order_ref, boundary_ref, grid_ref, legendre_ref, table_ref, inverse_ref, out_ref,
    legendre, table, inverse, got, keep, send, landed, stage, solved,
    load_sem, first_send, first_recv, second_send, second_recv, out_sem,
):
    slots, degrees, latitudes = legendre.shape
    columns = grid_ref.shape[2]
    band = grid_ref.shape[1]
    devices = landed.shape[1]
    share = landed.shape[2]
    tile = GROUP * share
    width = stage.shape[2]
    orders = stage.shape[1] // share
    ma = lax.axis_index("ma")
    row = lax.axis_index("row")
    me = ma * rows + row
    z = me // GROUP
    w = me % GROUP
    z_order = (GROUPS - 1 - z, (z + GROUPS // 2) % GROUPS, z + 1 - 2 * (z % 2), z)

    loads = [
        pltpu.make_async_copy(legendre_ref, legendre, load_sem.at[0]),
        pltpu.make_async_copy(table_ref, table, load_sem.at[1]),
        pltpu.make_async_copy(inverse_ref, inverse, load_sem.at[2]),
    ]
    for load in loads:
        load.start()

    barrier = pltpu.get_barrier_semaphore()

    @pl.loop(1, devices)
    def _(k):
        other = (me + k) % devices
        pl.semaphore_signal(
            barrier, inc=1, device_id=(other // rows, other % rows), device_id_type=MESH
        )

    pl.semaphore_wait(barrier, devices - 1)

    def to_slots(slot):
        here = got.at[
            slot,
            pl.ds(pl.multiple_of(ma * band, 16), band),
            pl.ds(pl.multiple_of(row * columns, 128), columns),
        ]

        def send_to(other):
            pltpu.make_async_remote_copy(
                src_ref=grid_ref.at[other * slots + slot],
                dst_ref=here,
                send_sem=first_send.at[slot],
                recv_sem=first_recv.at[slot],
                device_id=(other // rows, other % rows),
                device_id_type=MESH,
            ).start()

        for place, there in enumerate(z_order):
            @pl.loop(0 if place < GROUPS - 1 else 1, GROUP)
            def _(k, there=there):
                send_to(there * GROUP + (w + k) % GROUP)

        pltpu.make_async_copy(
            grid_ref.at[me * slots + slot], here, first_recv.at[slot]
        ).start()

    for slot in range(slots):
        to_slots(slot)

    column = lax.broadcasted_iota(jnp.int32, keep.shape, 1)
    mode = column % width
    field = (column // width) % 2
    first = jnp.where(field == 0, boundary_ref[0, 0], boundary_ref[1, 0])
    last = jnp.where(field == 0, boundary_ref[0, 1], boundary_ref[1, 1])
    keep[...] = jnp.where((mode == first) | (mode == last), 0.0, 1.0)

    def analyse(slot, there):
        start = pl.multiple_of(there * tile, tile)
        spectrum = jnp.dot(
            legendre[slot, pl.ds(start, tile), :], got[slot], preferred_element_type=jnp.float32
        )
        degree = start + lax.broadcasted_iota(jnp.int32, spectrum.shape, 0)
        spectrum = jnp.where(degree >= order_ref[slot], spectrum, 0.0)
        high = spectrum.astype(jnp.bfloat16)
        low = (spectrum - high.astype(jnp.float32)).astype(jnp.bfloat16)
        right = jnp.dot(high, table[0], preferred_element_type=jnp.float32)
        right += jnp.dot(low, table[0], preferred_element_type=jnp.float32)
        right += jnp.dot(high, table[1], preferred_element_type=jnp.float32)
        right = jnp.where(keep[0:1, :] > 0.0, right, 0.0)
        send[slot, pl.ds(start, tile), :] = right.astype(jnp.bfloat16)

    def piece(slot, other):
        return send.at[slot, pl.ds(pl.multiple_of(other * share, share), share)]

    def to_degrees(slot, there, own):
        @pl.loop(1 if own else 0, GROUP)
        def _(k):
            other = there * GROUP + (w + k) % GROUP
            pltpu.make_async_remote_copy(
                src_ref=piece(slot, other),
                dst_ref=landed.at[slot, me],
                send_sem=second_send.at[slot],
                recv_sem=second_recv.at[slot],
                device_id=(other // rows, other % rows),
                device_id_type=MESH,
            ).start()

        if own:
            pltpu.make_async_copy(
                piece(slot, me), landed.at[slot, me], second_recv.at[slot]
            ).start()

    def wait_bytes(ref, sem):
        pltpu.make_async_copy(ref, ref, sem).wait()

    loads[0].wait()
    loads[1].wait()
    upper = z >= GROUPS // 2
    wait_bytes(got.at[0], first_recv.at[0])
    for place, there in enumerate(z_order):
        analyse(0, there)
        to_degrees(0, there, place == GROUPS - 1)
    wait_bytes(got.at[1], first_recv.at[1])
    for place, there in enumerate(z_order):
        @pl.when(there >= GROUPS // 2)
        def _(place=place, there=there):
            analyse(1, there)
            to_degrees(1, there, place == GROUPS - 1)

    def put(slot, source, value):
        for part in range(2):
            for q in range(2):
                at = (2 * part + q) * width
                stage[
                    q, pl.ds(source * 2 * slots + 2 * slot + part, share, stride=orders), :
                ] = value[:, at:at + width]

    def gather(slot):
        @pl.loop(0, devices)
        def _(source):
            put(slot, source, landed[slot, source].astype(jnp.float32))

    wait_bytes(landed.at[0], second_recv.at[0])
    gather(0)

    @pl.when(upper)
    def _():
        wait_bytes(landed.at[1], second_recv.at[1])
        gather(1)

    @pl.when(jnp.logical_not(upper))
    def _():
        @pl.loop(0, devices)
        def _(source):
            put(1, source, jnp.zeros((share, 4 * width), jnp.float32))

    loads[2].wait()

    @pl.loop(0, share)
    def _(l):
        at = pl.ds(pl.multiple_of(l * orders, orders), orders)
        right = jnp.concatenate([stage[0, at, :], stage[1, at, :]], axis=1).astype(jnp.bfloat16)
        solved[l] = lax.dot_general(
            inverse[l], right, (((1,), (1,)), ((), ())), preferred_element_type=jnp.float32
        ).astype(jnp.bfloat16)

    result = pltpu.make_async_copy(solved, out_ref, out_sem)
    result.start()
    for slot in range(slots):
        wait_bytes(grid_ref.at[pl.ds(0, devices - 1)], first_send.at[slot])
    wait_bytes(send.at[0, pl.ds(0, (devices - 1) * share)], second_send.at[0])

    @pl.when(upper)
    def _():
        wait_bytes(send.at[1, pl.ds(0, (devices // 2 - 1) * share)], second_send.at[1])

    @pl.when(jnp.logical_not(upper))
    def _():
        wait_bytes(send.at[1, pl.ds(0, devices // 2 * share)], second_send.at[1])

    result.wait()


def on_device(grid_field, legendre, order_table, boundary_rows, inverse):
    rows = lax.axis_size("row")
    devices = lax.axis_size("ma") * rows
    slots, degrees, latitudes = legendre.shape
    band, columns = grid_field.shape[1:]
    share = degrees // devices
    full_width = columns * rows
    orders = 2 * slots * devices
    fits = (
        devices == GROUP * GROUPS and slots == 2 and share % 16 == 0 and band % 16 == 0
        and columns % 128 == 0 and full_width == 512
    )
    if not fits:
        return with_collectives(grid_field, legendre, order_table, boundary_rows, inverse)
    width = full_width // 4
    any_space = pl.BlockSpec(memory_space=pl.ANY)
    scalars = pl.BlockSpec(memory_space=pltpu.SMEM)
    dma = pltpu.SemaphoreType.DMA
    return pl.pallas_call(
        functools.partial(kernel, rows),
        out_shape=jax.ShapeDtypeStruct((share, 2 * width, orders), jnp.bfloat16),
        in_specs=[scalars, scalars, any_space, any_space, any_space, any_space],
        out_specs=any_space,
        scratch_shapes=[
            pltpu.VMEM(legendre.shape, jnp.bfloat16),
            pltpu.VMEM((2, full_width, full_width), jnp.bfloat16),
            pltpu.VMEM(inverse.shape, jnp.bfloat16),
            pltpu.VMEM((slots, latitudes, full_width), jnp.bfloat16),
            pltpu.VMEM((8, full_width), jnp.float32),
            pltpu.VMEM((slots, degrees, full_width), jnp.bfloat16),
            pltpu.VMEM((slots, devices, share, full_width), jnp.bfloat16),
            pltpu.VMEM((2, share * orders, width), jnp.float32),
            pltpu.VMEM((share, 2 * width, orders), jnp.bfloat16),
            dma((3,)), dma((slots,)), dma((slots,)), dma((slots,)), dma((slots,)), dma,
        ],
        compiler_params=pltpu.CompilerParams(
            collective_id=0, has_side_effects=True, vmem_limit_bytes=44 * 2 ** 20
        ),
        cost_estimate=pl.CostEstimate(
            flops=6 * 10 ** 9, bytes_accessed=18 * 2 ** 20, transcendentals=0
        ),
    )(order_table, boundary_rows, grid_field, legendre, radial_parts(width), inverse)


def solution(mesh):
    return jax.shard_map(
        on_device,
        mesh=mesh,
        in_specs=(
            P(None, "ma", "row"),
            P(("ma", "row"), None, None),
            P(("ma", "row")),
            P(),
            P(("ma", "row"), None, None),
        ),
        out_specs=P(("ma", "row"), None, None),
        check_vma=False,
    )
```

```python
import functools

import jax
import jax.numpy as jnp
import numpy as np
from jax import lax
from jax.experimental import pallas as pl
from jax.experimental.pallas import tpu as pltpu
from jax.sharding import PartitionSpec as P

MESH = pl.DeviceIdType.MESH
GROUP = 8
GROUPS = 4


def chebyshev_table(radial_levels):
    wave_number = jnp.arange(radial_levels, dtype=jnp.float32)[:, None]
    grid_point = jnp.arange(radial_levels, dtype=jnp.float32)[None, :]
    cos_table = jnp.cos(jnp.pi * wave_number * (grid_point + 0.5) / radial_levels) * jnp.sqrt(
        2.0 / radial_levels
    )
    return jnp.where(wave_number == 0.0, cos_table * jnp.sqrt(0.5), cos_table)


def boundary_keep(boundary_rows, radial_levels):
    row_index = jnp.arange(radial_levels, dtype=jnp.int32)[None, :]
    boundary_hit = (row_index == boundary_rows[:, 0:1]) | (row_index == boundary_rows[:, 1:2])
    return jnp.where(boundary_hit, 0.0, 1.0).astype(jnp.float32)


def radial_matrix(boundary_rows, radial_levels):
    cheb = chebyshev_table(radial_levels)
    keep = boundary_keep(boundary_rows, radial_levels)
    eye = jnp.eye(2, dtype=jnp.float32)
    full = (
        cheb.T[:, None, None, None, None, :]
        * eye[None, :, None, None, :, None]
        * eye[None, None, :, :, None, None]
        * keep[None, None, None, None, :, :]
    )
    return full.reshape(4 * radial_levels, 4 * radial_levels)


def with_collectives(grid_field, legendre, order_table, boundary_rows, inverse):
    ma_count = lax.axis_size("ma")
    row_count = lax.axis_size("row")
    devices = ma_count * row_count
    slots, degree_total, latitudes = legendre.shape
    columns = grid_field.shape[2]
    radial_levels = columns * row_count // 4
    share = degree_total // devices
    got = lax.all_to_all(
        grid_field.reshape(devices, slots, latitudes // ma_count, columns),
        ("ma", "row"), split_axis=0, concat_axis=0, tiled=True,
    )
    got = got.reshape(ma_count, row_count, slots, latitudes // ma_count, columns)
    got = got.transpose(2, 0, 3, 1, 4).reshape(slots, latitudes, row_count * columns)
    spectrum = jnp.einsum("xlt,xtd->xld", legendre, got, preferred_element_type=jnp.float32)
    degrees = jnp.arange(degree_total, dtype=jnp.int32)
    lower = degrees[None, :] >= order_table[:, None]
    spectrum = jnp.where(lower[:, :, None], spectrum, 0.0)
    matrix = radial_matrix(boundary_rows, radial_levels)
    matrix_high = matrix.astype(jnp.bfloat16)
    matrix_low = (matrix - matrix_high.astype(jnp.float32)).astype(jnp.bfloat16)
    high = spectrum.astype(jnp.bfloat16)
    low = (spectrum - high.astype(jnp.float32)).astype(jnp.bfloat16)

    def mul(a, b):
        return jnp.einsum("xld,de->xle", a, b, preferred_element_type=jnp.float32)

    right = mul(high, matrix_high) + (mul(low, matrix_high) + mul(high, matrix_low))
    right = right.astype(jnp.bfloat16).reshape(slots, degree_total, 2, 2 * radial_levels)
    right = right.transpose(1, 0, 2, 3).reshape(devices, share, 2 * slots, 2 * radial_levels)
    right = lax.all_to_all(right, ("ma", "row"), split_axis=0, concat_axis=0, tiled=True)
    right = right.transpose(1, 0, 2, 3).reshape(share, devices * 2 * slots, 2 * radial_levels)
    solved = jnp.einsum("lij,lnj->lin", inverse, right, preferred_element_type=jnp.float32)
    return solved.astype(jnp.bfloat16)


def radial_parts(radial_levels):
    wave_number = np.arange(radial_levels, dtype=np.float64)[:, None]
    point = np.arange(radial_levels, dtype=np.float64)[None, :] + 0.5
    cheb = np.cos(np.pi * wave_number * point / radial_levels) * np.sqrt(2.0 / radial_levels)
    cheb[0] *= np.sqrt(0.5)
    full = np.zeros((radial_levels, 2, 2, 2, 2, radial_levels), np.float32)
    for q in range(2):
        for p in range(2):
            full[:, q, p, p, q, :] = cheb.T
    full = full.reshape(4 * radial_levels, 4 * radial_levels)
    return full


def kernel(
    rows, order_hbm, boundary_hbm, grid_ref, legendre_ref, table_hbm, inverse_ref, out_ref,
    order_ref, boundary_ref, table_ref,
    legendre, table, inverse, got, keep, send, landed, stage, solved,
    load_sem, first_send, first_recv, second_send, second_recv, out_sem,
):
    slots, degrees, latitudes = legendre.shape
    columns = grid_ref.shape[2]
    band = grid_ref.shape[1]
    devices = landed.shape[1]
    share = landed.shape[2]
    tile = GROUP * share
    width = stage.shape[2]
    orders = stage.shape[1] // share
    ma = lax.axis_index("ma")
    row = lax.axis_index("row")
    me = ma * rows + row
    z = me // GROUP
    w = me % GROUP
    z_order = (GROUPS - 1 - z, (z + GROUPS // 2) % GROUPS, z + 1 - 2 * (z % 2), z)
    z_mixed = (z_order[0], z_order[2], z_order[1], z_order[3])

    loads = [
        pltpu.make_async_copy(legendre_ref, legendre, load_sem.at[0]),
        pltpu.make_async_copy(table_hbm, table_ref, load_sem.at[1]),
        pltpu.make_async_copy(inverse_ref, inverse, load_sem.at[2]),
        pltpu.make_async_copy(order_hbm, order_ref, load_sem.at[3]),
        pltpu.make_async_copy(boundary_hbm, boundary_ref, load_sem.at[4]),
    ]
    for load in loads:
        load.start()

    barrier = pltpu.get_barrier_semaphore()

    @pl.loop(1, devices)
    def _(k):
        other = (me + k) % devices
        pl.semaphore_signal(
            barrier, inc=1, device_id=(other // rows, other % rows), device_id_type=MESH
        )

    pl.semaphore_wait(barrier, devices - 1)

    def to_slots(slot):
        here = got.at[
            slot,
            pl.ds(pl.multiple_of(ma * band, 16), band),
            pl.ds(pl.multiple_of(row * columns, 128), columns),
        ]

        def send_to(other):
            pltpu.make_async_remote_copy(
                src_ref=grid_ref.at[other * slots + slot],
                dst_ref=here,
                send_sem=first_send.at[slot],
                recv_sem=first_recv.at[slot],
                device_id=(other // rows, other % rows),
                device_id_type=MESH,
            ).start()

        @pl.loop(1, GROUP)
        def _(k):
            for there in z_mixed:
                send_to(there * GROUP + (w + k) % GROUP)

        for there in z_mixed[:-1]:
            send_to(there * GROUP + w)

        pltpu.make_async_copy(
            grid_ref.at[me * slots + slot], here, first_recv.at[slot]
        ).start()

    for slot in range(slots):
        to_slots(slot)

    for load in loads[1:]:
        load.wait()
    full = table_ref[...]
    table[0] = full.astype(jnp.bfloat16)
    table[1] = (full - table[0].astype(jnp.float32)).astype(jnp.bfloat16)
    column = lax.broadcasted_iota(jnp.int32, keep.shape, 1)
    mode = column % width
    field = (column // width) % 2
    first = jnp.where(field == 0, boundary_ref[0, 0], boundary_ref[1, 0])
    last = jnp.where(field == 0, boundary_ref[0, 1], boundary_ref[1, 1])
    keep[...] = jnp.where((mode == first) | (mode == last), 0.0, 1.0)

    def analyse(slot, there):
        start = pl.multiple_of(there * tile, tile)
        spectrum = jnp.dot(
            legendre[slot, pl.ds(start, tile), :], got[slot], preferred_element_type=jnp.float32
        )
        degree = start + lax.broadcasted_iota(jnp.int32, spectrum.shape, 0)
        spectrum = jnp.where(degree >= order_ref[slot], spectrum, 0.0)
        high = spectrum.astype(jnp.bfloat16)
        low = (spectrum - high.astype(jnp.float32)).astype(jnp.bfloat16)
        right = jnp.dot(high, table[0], preferred_element_type=jnp.float32)
        right += jnp.dot(low, table[0], preferred_element_type=jnp.float32)
        right += jnp.dot(high, table[1], preferred_element_type=jnp.float32)
        right = jnp.where(keep[0:1, :] > 0.0, right, 0.0)
        send[slot, pl.ds(start, tile), :] = right.astype(jnp.bfloat16)

    def piece(slot, other):
        return send.at[slot, pl.ds(pl.multiple_of(other * share, share), share)]

    def to_degree(slot, other):
        pltpu.make_async_remote_copy(
            src_ref=piece(slot, other),
            dst_ref=landed.at[slot, me],
            send_sem=second_send.at[slot],
            recv_sem=second_recv.at[slot, z],
            device_id=(other // rows, other % rows),
            device_id_type=MESH,
        ).start()

    def keep_own(slot):
        pltpu.make_async_copy(
            piece(slot, me), landed.at[slot, me], second_recv.at[slot, z]
        ).start()

    def wait_bytes(ref, sem):
        pltpu.make_async_copy(ref, ref, sem).wait()

    loads[0].wait()
    upper = z >= GROUPS // 2
    wait_bytes(got.at[0], first_recv.at[0])
    for there in z_order:
        analyse(0, there)

    @pl.loop(1, GROUP)
    def _(k):
        for there in z_mixed:
            to_degree(0, there * GROUP + (w + k) % GROUP)

    for there in z_mixed[:-1]:
        to_degree(0, there * GROUP + w)
    keep_own(0)
    wait_bytes(got.at[1], first_recv.at[1])
    for place, there in enumerate(z_order):
        @pl.when(there >= GROUPS // 2)
        def _(place=place, there=there):
            own = place == GROUPS - 1
            analyse(1, there)

            @pl.loop(1 if own else 0, GROUP)
            def _(k):
                to_degree(1, there * GROUP + (w + k) % GROUP)

            if own:
                keep_own(1)

    def put(slot, source, value):
        for part in range(2):
            for q in range(2):
                at = (2 * part + q) * width
                stage[
                    q, pl.ds(source * 2 * slots + 2 * slot + part, share, stride=orders), :
                ] = value[:, at:at + width]

    def gather(slot):
        for source_z in z_order[::-1]:
            part = pl.ds(source_z * GROUP, GROUP)
            wait_bytes(landed.at[slot, part], second_recv.at[slot, source_z])

            @pl.loop(0, GROUP)
            def _(k):
                source = source_z * GROUP + k
                put(slot, source, landed[slot, source].astype(jnp.float32))

    @pl.when(jnp.logical_not(upper))
    def _():
        @pl.loop(0, devices)
        def _(source):
            put(1, source, jnp.zeros((share, 4 * width), jnp.float32))

    gather(0)

    @pl.when(upper)
    def _():
        gather(1)

    some = share // 4

    @pl.loop(0, 4)
    def _(step):
        @pl.loop(0, some, unroll=4)
        def _(k):
            l = step * some + k
            at = pl.ds(pl.multiple_of(l * orders, orders), orders)
            right = jnp.concatenate([stage[0, at, :], stage[1, at, :]], axis=1)
            solved[l] = lax.dot_general(
                inverse[l], right.astype(jnp.bfloat16), (((1,), (1,)), ((), ())),
                preferred_element_type=jnp.float32,
            ).astype(jnp.bfloat16)

        done = pl.ds(step * some, some)
        pltpu.make_async_copy(solved.at[done], out_ref.at[done], out_sem).start()

    for slot in range(slots):
        wait_bytes(grid_ref.at[pl.ds(0, devices - 1)], first_send.at[slot])
    wait_bytes(send.at[0, pl.ds(0, (devices - 1) * share)], second_send.at[0])

    @pl.when(upper)
    def _():
        wait_bytes(send.at[1, pl.ds(0, (devices // 2 - 1) * share)], second_send.at[1])

    @pl.when(jnp.logical_not(upper))
    def _():
        wait_bytes(send.at[1, pl.ds(0, devices // 2 * share)], second_send.at[1])

    wait_bytes(solved, out_sem)


def on_device(grid_field, legendre, order_table, boundary_rows, inverse):
    rows = lax.axis_size("row")
    devices = lax.axis_size("ma") * rows
    slots, degrees, latitudes = legendre.shape
    band, columns = grid_field.shape[1:]
    share = degrees // devices
    full_width = columns * rows
    orders = 2 * slots * devices
    fits = (
        devices == GROUP * GROUPS and slots == 2 and share % 16 == 0 and band % 16 == 0
        and columns % 128 == 0 and full_width == 512
    )
    if not fits:
        return with_collectives(grid_field, legendre, order_table, boundary_rows, inverse)
    width = full_width // 4
    any_space = pl.BlockSpec(memory_space=pl.ANY)
    dma = pltpu.SemaphoreType.DMA
    return pl.pallas_call(
        functools.partial(kernel, rows),
        out_shape=jax.ShapeDtypeStruct((share, 2 * width, orders), jnp.bfloat16),
        in_specs=[any_space] * 6,
        out_specs=any_space,
        scratch_shapes=[
            pltpu.SMEM(order_table.shape, jnp.int32),
            pltpu.SMEM(boundary_rows.shape, jnp.int32),
            pltpu.VMEM((full_width, full_width), jnp.float32),
            pltpu.VMEM(legendre.shape, jnp.bfloat16),
            pltpu.VMEM((2, full_width, full_width), jnp.bfloat16),
            pltpu.VMEM(inverse.shape, jnp.bfloat16),
            pltpu.VMEM((slots, latitudes, full_width), jnp.bfloat16),
            pltpu.VMEM((8, full_width), jnp.float32),
            pltpu.VMEM((slots, degrees, full_width), jnp.bfloat16),
            pltpu.VMEM((slots, devices, share, full_width), jnp.bfloat16),
            pltpu.VMEM((2, share * orders, width), jnp.float32),
            pltpu.VMEM((share, 2 * width, orders), jnp.bfloat16),
            dma((5,)), dma((slots,)), dma((slots,)), dma((slots,)), dma((slots, GROUPS)), dma,
        ],
        compiler_params=pltpu.CompilerParams(
            collective_id=0, has_side_effects=True, vmem_limit_bytes=60 * 2 ** 20
        ),
        cost_estimate=pl.CostEstimate(
            flops=6 * 10 ** 9, bytes_accessed=18 * 2 ** 20, transcendentals=0
        ),
    )(order_table, boundary_rows, grid_field, legendre, radial_parts(width), inverse)


def solution(mesh):
    return jax.shard_map(
        on_device,
        mesh=mesh,
        in_specs=(
            P(None, "ma", "row"),
            P(("ma", "row"), None, None),
            P(("ma", "row")),
            P(),
            P(("ma", "row"), None, None),
        ),
        out_specs=P(("ma", "row"), None, None),
        check_vma=False,
    )
```

```python
import functools

import jax
import jax.numpy as jnp
import numpy as np
from jax import lax
from jax.experimental import pallas as pl
from jax.experimental.pallas import tpu as pltpu
from jax.sharding import PartitionSpec as P

MESH = pl.DeviceIdType.MESH
GROUP = 8
GROUPS = 4


def chebyshev_table(radial_levels):
    wave_number = jnp.arange(radial_levels, dtype=jnp.float32)[:, None]
    grid_point = jnp.arange(radial_levels, dtype=jnp.float32)[None, :]
    cos_table = jnp.cos(jnp.pi * wave_number * (grid_point + 0.5) / radial_levels) * jnp.sqrt(
        2.0 / radial_levels
    )
    return jnp.where(wave_number == 0.0, cos_table * jnp.sqrt(0.5), cos_table)


def boundary_keep(boundary_rows, radial_levels):
    row_index = jnp.arange(radial_levels, dtype=jnp.int32)[None, :]
    boundary_hit = (row_index == boundary_rows[:, 0:1]) | (row_index == boundary_rows[:, 1:2])
    return jnp.where(boundary_hit, 0.0, 1.0).astype(jnp.float32)


def radial_matrix(boundary_rows, radial_levels):
    cheb = chebyshev_table(radial_levels)
    keep = boundary_keep(boundary_rows, radial_levels)
    eye = jnp.eye(2, dtype=jnp.float32)
    full = (
        cheb.T[:, None, None, None, None, :]
        * eye[None, :, None, None, :, None]
        * eye[None, None, :, :, None, None]
        * keep[None, None, None, None, :, :]
    )
    return full.reshape(4 * radial_levels, 4 * radial_levels)


def with_collectives(grid_field, legendre, order_table, boundary_rows, inverse):
    ma_count = lax.axis_size("ma")
    row_count = lax.axis_size("row")
    devices = ma_count * row_count
    slots, degree_total, latitudes = legendre.shape
    columns = grid_field.shape[2]
    radial_levels = columns * row_count // 4
    share = degree_total // devices
    got = lax.all_to_all(
        grid_field.reshape(devices, slots, latitudes // ma_count, columns),
        ("ma", "row"), split_axis=0, concat_axis=0, tiled=True,
    )
    got = got.reshape(ma_count, row_count, slots, latitudes // ma_count, columns)
    got = got.transpose(2, 0, 3, 1, 4).reshape(slots, latitudes, row_count * columns)
    spectrum = jnp.einsum("xlt,xtd->xld", legendre, got, preferred_element_type=jnp.float32)
    degrees = jnp.arange(degree_total, dtype=jnp.int32)
    lower = degrees[None, :] >= order_table[:, None]
    spectrum = jnp.where(lower[:, :, None], spectrum, 0.0)
    matrix = radial_matrix(boundary_rows, radial_levels)
    matrix_high = matrix.astype(jnp.bfloat16)
    matrix_low = (matrix - matrix_high.astype(jnp.float32)).astype(jnp.bfloat16)
    high = spectrum.astype(jnp.bfloat16)
    low = (spectrum - high.astype(jnp.float32)).astype(jnp.bfloat16)

    def mul(a, b):
        return jnp.einsum("xld,de->xle", a, b, preferred_element_type=jnp.float32)

    right = mul(high, matrix_high) + (mul(low, matrix_high) + mul(high, matrix_low))
    right = right.astype(jnp.bfloat16).reshape(slots, degree_total, 2, 2 * radial_levels)
    right = right.transpose(1, 0, 2, 3).reshape(devices, share, 2 * slots, 2 * radial_levels)
    right = lax.all_to_all(right, ("ma", "row"), split_axis=0, concat_axis=0, tiled=True)
    right = right.transpose(1, 0, 2, 3).reshape(share, devices * 2 * slots, 2 * radial_levels)
    solved = jnp.einsum("lij,lnj->lin", inverse, right, preferred_element_type=jnp.float32)
    return solved.astype(jnp.bfloat16)


def radial_parts(radial_levels):
    wave_number = np.arange(radial_levels, dtype=np.float64)[:, None]
    point = np.arange(radial_levels, dtype=np.float64)[None, :] + 0.5
    cheb = np.cos(np.pi * wave_number * point / radial_levels) * np.sqrt(2.0 / radial_levels)
    cheb[0] *= np.sqrt(0.5)
    full = np.zeros((radial_levels, 2, 2, 2, 2, radial_levels), np.float32)
    for q in range(2):
        for p in range(2):
            full[:, q, p, p, q, :] = cheb.T
    full = full.reshape(4 * radial_levels, 4 * radial_levels)
    return full


def kernel(
    rows, order_hbm, boundary_hbm, grid_ref, legendre_ref, table_hbm, inverse_ref, out_ref,
    order_ref, boundary_ref, table_ref,
    legendre, table, inverse, got, keep, send, landed, stage, solved,
    load_sem, first_send, first_recv, second_send, second_recv, out_sem,
):
    slots, degrees, latitudes = legendre.shape
    columns = grid_ref.shape[2]
    band = grid_ref.shape[1]
    devices = landed.shape[1]
    share = landed.shape[2]
    tile = GROUP * share
    width = stage.shape[2]
    orders = stage.shape[1] // share
    ma = lax.axis_index("ma")
    row = lax.axis_index("row")
    me = ma * rows + row
    z = me // GROUP
    w = me % GROUP
    z_order = (GROUPS - 1 - z, (z + GROUPS // 2) % GROUPS, z + 1 - 2 * (z % 2), z)
    z_mixed = (z_order[0], z_order[2], z_order[1], z_order[3])

    loads = [
        pltpu.make_async_copy(legendre_ref, legendre, load_sem.at[0]),
        pltpu.make_async_copy(table_hbm, table_ref, load_sem.at[1]),
        pltpu.make_async_copy(inverse_ref, inverse, load_sem.at[2]),
        pltpu.make_async_copy(order_hbm, order_ref, load_sem.at[3]),
        pltpu.make_async_copy(boundary_hbm, boundary_ref, load_sem.at[4]),
    ]
    for load in loads:
        load.start()

    barrier = pltpu.get_barrier_semaphore()

    @pl.loop(1, devices)
    def _(k):
        other = (me + k) % devices
        pl.semaphore_signal(
            barrier, inc=1, device_id=(other // rows, other % rows), device_id_type=MESH
        )

    pl.semaphore_wait(barrier, devices - 1)

    def to_slots(slot):
        here = got.at[slot, row, pl.ds(pl.multiple_of(ma * band, 16), band)]

        def send_to(other):
            pltpu.make_async_remote_copy(
                src_ref=grid_ref.at[other * slots + slot],
                dst_ref=here,
                send_sem=first_send.at[slot],
                recv_sem=first_recv.at[slot],
                device_id=(other // rows, other % rows),
                device_id_type=MESH,
            ).start()

        @pl.loop(1, GROUP)
        def _(k):
            for there in z_mixed:
                send_to(there * GROUP + (w + k) % GROUP)

        for there in z_mixed[:-1]:
            send_to(there * GROUP + w)

        pltpu.make_async_copy(
            grid_ref.at[me * slots + slot], here, first_recv.at[slot]
        ).start()

    for slot in range(slots):
        to_slots(slot)

    for load in loads[1:]:
        load.wait()
    full = table_ref[...]
    table[0] = full.astype(jnp.bfloat16)
    table[1] = (full - table[0].astype(jnp.float32)).astype(jnp.bfloat16)
    column = lax.broadcasted_iota(jnp.int32, keep.shape, 1)
    mode = column % width
    field = (column // width) % 2
    first = jnp.where(field == 0, boundary_ref[0, 0], boundary_ref[1, 0])
    last = jnp.where(field == 0, boundary_ref[0, 1], boundary_ref[1, 1])
    keep[...] = jnp.where((mode == first) | (mode == last), 0.0, 1.0)

    def analyse(slot, there):
        start = pl.multiple_of(there * tile, tile)
        grid = jnp.concatenate([got[slot, band_row] for band_row in range(rows)], axis=1)
        spectrum = jnp.dot(
            legendre[slot, pl.ds(start, tile), :], grid, preferred_element_type=jnp.float32
        )
        degree = start + lax.broadcasted_iota(jnp.int32, spectrum.shape, 0)
        spectrum = jnp.where(degree >= order_ref[slot], spectrum, 0.0)
        high = spectrum.astype(jnp.bfloat16)
        low = (spectrum - high.astype(jnp.float32)).astype(jnp.bfloat16)
        right = jnp.dot(high, table[0], preferred_element_type=jnp.float32)
        right += jnp.dot(low, table[0], preferred_element_type=jnp.float32)
        right += jnp.dot(high, table[1], preferred_element_type=jnp.float32)
        right = jnp.where(keep[0:1, :] > 0.0, right, 0.0)
        send[slot, pl.ds(start, tile), :] = right.astype(jnp.bfloat16)

    def piece(slot, other, at, count):
        return send.at[slot, pl.ds(pl.multiple_of(other * share + at, 16), count)]

    def to_degree(slot, other, half):
        at, count = (0, share) if half is None else (half * (share // 2), share // 2)
        sem = second_recv.at[slot, half or 0, z]
        here = landed.at[slot, me, pl.ds(at, count)]
        return piece(slot, other, at, count), here, sem

    def copy_to(slot, other, half=None):
        source, here, sem = to_degree(slot, other, half)
        pltpu.make_async_remote_copy(
            src_ref=source,
            dst_ref=here,
            send_sem=second_send.at[slot],
            recv_sem=sem,
            device_id=(other // rows, other % rows),
            device_id_type=MESH,
        ).start()

    def keep_own(slot, half=None):
        source, here, sem = to_degree(slot, me, half)
        pltpu.make_async_copy(source, here, sem).start()

    def wait_bytes(ref, sem):
        pltpu.make_async_copy(ref, ref, sem).wait()

    loads[0].wait()
    upper = z >= GROUPS // 2
    wait_bytes(got.at[0], first_recv.at[0])
    far, near, next_far, own = z_mixed
    analyse(0, far)

    @pl.loop(0, GROUP)
    def _(k):
        copy_to(0, far * GROUP + (w + k) % GROUP)

    analyse(0, next_far)
    analyse(0, near)

    @pl.loop(0, GROUP)
    def _(k):
        for there in (next_far, near):
            copy_to(0, there * GROUP + (w + k) % GROUP)

    analyse(0, own)

    @pl.loop(1, GROUP)
    def _(k):
        copy_to(0, own * GROUP + (w + k) % GROUP)

    keep_own(0)
    wait_bytes(got.at[1], first_recv.at[1])
    up = z // (GROUPS // 2)
    one = far + up * (near - far)
    two = next_far + up * (own - next_far)

    def copy_half(there, skip, half):
        @pl.loop(skip, GROUP)
        def _(k):
            copy_to(1, there * GROUP + (w + k) % GROUP, half)

    analyse(1, one)
    copy_half(one, 0, 0)
    analyse(1, two)
    copy_half(two, up, 0)
    copy_half(one, 0, 1)
    copy_half(two, up, 1)

    @pl.when(upper)
    def _():
        keep_own(1, 0)
        keep_own(1, 1)

    def put(slot, source, at, value):
        for part in range(2):
            for q in range(2):
                first_row = at * orders + source * 2 * slots + 2 * slot + part
                column = (2 * part + q) * width
                stage[q, pl.ds(first_row, value.shape[0], stride=orders), :] = value[
                    :, column:column + width
                ]

    def gather(slot, half=None):
        at, count = (0, share) if half is None else (half * (share // 2), share // 2)
        for source_z in z_order[::-1]:
            part = landed.at[slot, pl.ds(source_z * GROUP, GROUP), pl.ds(at, count)]
            wait_bytes(part, second_recv.at[slot, half or 0, source_z])

            @pl.loop(0, GROUP)
            def _(k):
                source = source_z * GROUP + k
                put(slot, source, at, landed[slot, source, at:at + count].astype(jnp.float32))

    @pl.when(jnp.logical_not(upper))
    def _():
        @pl.loop(0, devices)
        def _(source):
            put(1, source, 0, jnp.zeros((share, 4 * width), jnp.float32))

    gather(0)
    some = share // 4
    for step in range(4):
        if step % 2 == 0:
            @pl.when(upper)
            def _(step=step):
                gather(1, step // 2)

        @pl.loop(0, some, unroll=4)
        def _(k, step=step):
            l = step * some + k
            at = pl.ds(pl.multiple_of(l * orders, orders), orders)
            right = jnp.concatenate([stage[0, at, :], stage[1, at, :]], axis=1)
            solved[l] = lax.dot_general(
                inverse[l], right.astype(jnp.bfloat16), (((1,), (1,)), ((), ())),
                preferred_element_type=jnp.float32,
            ).astype(jnp.bfloat16)

        done = pl.ds(step * some, some)
        pltpu.make_async_copy(solved.at[done], out_ref.at[done], out_sem).start()

    for slot in range(slots):
        wait_bytes(grid_ref.at[pl.ds(0, devices - 1)], first_send.at[slot])
    wait_bytes(send.at[0, pl.ds(0, (devices - 1) * share)], second_send.at[0])

    @pl.when(upper)
    def _():
        wait_bytes(send.at[1, pl.ds(0, (devices // 2 - 1) * share)], second_send.at[1])

    @pl.when(jnp.logical_not(upper))
    def _():
        wait_bytes(send.at[1, pl.ds(0, devices // 2 * share)], second_send.at[1])

    wait_bytes(solved, out_sem)


def on_device(grid_field, legendre, order_table, boundary_rows, inverse):
    rows = lax.axis_size("row")
    devices = lax.axis_size("ma") * rows
    slots, degrees, latitudes = legendre.shape
    band, columns = grid_field.shape[1:]
    share = degrees // devices
    full_width = columns * rows
    orders = 2 * slots * devices
    fits = (
        devices == GROUP * GROUPS and slots == 2 and share % 32 == 0 and band % 16 == 0
        and columns % 128 == 0 and full_width == 512
    )
    if not fits:
        return with_collectives(grid_field, legendre, order_table, boundary_rows, inverse)
    width = full_width // 4
    any_space = pl.BlockSpec(memory_space=pl.ANY)
    dma = pltpu.SemaphoreType.DMA
    operands = (
        order_table, boundary_rows, grid_field, legendre, jnp.asarray(radial_parts(width)), inverse
    )
    operands = [pltpu.with_memory_space_constraint(each, pltpu.HBM) for each in operands]
    return pl.pallas_call(
        functools.partial(kernel, rows),
        out_shape=jax.ShapeDtypeStruct((share, 2 * width, orders), jnp.bfloat16),
        in_specs=[pl.BlockSpec(memory_space=pltpu.HBM)] * 6,
        out_specs=any_space,
        scratch_shapes=[
            pltpu.SMEM(order_table.shape, jnp.int32),
            pltpu.SMEM(boundary_rows.shape, jnp.int32),
            pltpu.VMEM((full_width, full_width), jnp.float32),
            pltpu.VMEM(legendre.shape, jnp.bfloat16),
            pltpu.VMEM((2, full_width, full_width), jnp.bfloat16),
            pltpu.VMEM(inverse.shape, jnp.bfloat16),
            pltpu.VMEM((slots, rows, latitudes, columns), jnp.bfloat16),
            pltpu.VMEM((8, full_width), jnp.float32),
            pltpu.VMEM((slots, degrees, full_width), jnp.bfloat16),
            pltpu.VMEM((slots, devices, share, full_width), jnp.bfloat16),
            pltpu.VMEM((2, share * orders, width), jnp.float32),
            pltpu.VMEM((share, 2 * width, orders), jnp.bfloat16),
            dma((5,)), dma((slots,)), dma((slots,)), dma((slots,)), dma((slots, 2, GROUPS)), dma,
        ],
        compiler_params=pltpu.CompilerParams(
            collective_id=0, has_side_effects=True, vmem_limit_bytes=44 * 2 ** 20
        ),
        cost_estimate=pl.CostEstimate(
            flops=6 * 10 ** 9, bytes_accessed=18 * 2 ** 20, transcendentals=0
        ),
    )(*operands)


def solution(mesh):
    return jax.shard_map(
        on_device,
        mesh=mesh,
        in_specs=(
            P(None, "ma", "row"),
            P(("ma", "row"), None, None),
            P(("ma", "row")),
            P(),
            P(("ma", "row"), None, None),
        ),
        out_specs=P(("ma", "row"), None, None),
        check_vma=False,
    )
```

```python
import functools

import jax
import jax.numpy as jnp
import numpy as np
from jax import lax
from jax.experimental import pallas as pl
from jax.experimental.pallas import tpu as pltpu
from jax.sharding import PartitionSpec as P

MESH = pl.DeviceIdType.MESH
GROUP = 8
GROUPS = 4


def chebyshev_table(radial_levels):
    wave_number = jnp.arange(radial_levels, dtype=jnp.float32)[:, None]
    grid_point = jnp.arange(radial_levels, dtype=jnp.float32)[None, :]
    cos_table = jnp.cos(jnp.pi * wave_number * (grid_point + 0.5) / radial_levels) * jnp.sqrt(
        2.0 / radial_levels
    )
    return jnp.where(wave_number == 0.0, cos_table * jnp.sqrt(0.5), cos_table)


def boundary_keep(boundary_rows, radial_levels):
    row_index = jnp.arange(radial_levels, dtype=jnp.int32)[None, :]
    boundary_hit = (row_index == boundary_rows[:, 0:1]) | (row_index == boundary_rows[:, 1:2])
    return jnp.where(boundary_hit, 0.0, 1.0).astype(jnp.float32)


def radial_matrix(boundary_rows, radial_levels):
    cheb = chebyshev_table(radial_levels)
    keep = boundary_keep(boundary_rows, radial_levels)
    eye = jnp.eye(2, dtype=jnp.float32)
    full = (
        cheb.T[:, None, None, None, None, :]
        * eye[None, :, None, None, :, None]
        * eye[None, None, :, :, None, None]
        * keep[None, None, None, None, :, :]
    )
    return full.reshape(4 * radial_levels, 4 * radial_levels)


def with_collectives(grid_field, legendre, order_table, boundary_rows, inverse):
    ma_count = lax.axis_size("ma")
    row_count = lax.axis_size("row")
    devices = ma_count * row_count
    slots, degree_total, latitudes = legendre.shape
    columns = grid_field.shape[2]
    radial_levels = columns * row_count // 4
    share = degree_total // devices
    got = lax.all_to_all(
        grid_field.reshape(devices, slots, latitudes // ma_count, columns),
        ("ma", "row"), split_axis=0, concat_axis=0, tiled=True,
    )
    got = got.reshape(ma_count, row_count, slots, latitudes // ma_count, columns)
    got = got.transpose(2, 0, 3, 1, 4).reshape(slots, latitudes, row_count * columns)
    spectrum = jnp.einsum("xlt,xtd->xld", legendre, got, preferred_element_type=jnp.float32)
    degrees = jnp.arange(degree_total, dtype=jnp.int32)
    lower = degrees[None, :] >= order_table[:, None]
    spectrum = jnp.where(lower[:, :, None], spectrum, 0.0)
    matrix = radial_matrix(boundary_rows, radial_levels)
    matrix_high = matrix.astype(jnp.bfloat16)
    matrix_low = (matrix - matrix_high.astype(jnp.float32)).astype(jnp.bfloat16)
    high = spectrum.astype(jnp.bfloat16)
    low = (spectrum - high.astype(jnp.float32)).astype(jnp.bfloat16)

    def mul(a, b):
        return jnp.einsum("xld,de->xle", a, b, preferred_element_type=jnp.float32)

    right = mul(high, matrix_high) + (mul(low, matrix_high) + mul(high, matrix_low))
    right = right.astype(jnp.bfloat16).reshape(slots, degree_total, 2, 2 * radial_levels)
    right = right.transpose(1, 0, 2, 3).reshape(devices, share, 2 * slots, 2 * radial_levels)
    right = lax.all_to_all(right, ("ma", "row"), split_axis=0, concat_axis=0, tiled=True)
    right = right.transpose(1, 0, 2, 3).reshape(share, devices * 2 * slots, 2 * radial_levels)
    solved = jnp.einsum("lij,lnj->lin", inverse, right, preferred_element_type=jnp.float32)
    return solved.astype(jnp.bfloat16)


def radial_parts(radial_levels):
    wave_number = np.arange(radial_levels, dtype=np.float64)[:, None]
    point = np.arange(radial_levels, dtype=np.float64)[None, :] + 0.5
    cheb = np.cos(np.pi * wave_number * point / radial_levels) * np.sqrt(2.0 / radial_levels)
    cheb[0] *= np.sqrt(0.5)
    full = np.zeros((radial_levels, 2, 2, 2, 2, radial_levels), np.float32)
    for q in range(2):
        for p in range(2):
            full[:, q, p, p, q, :] = cheb.T
    full = full.reshape(4 * radial_levels, 4 * radial_levels)
    return full


def kernel(
    rows, order_hbm, boundary_hbm, grid_ref, legendre_ref, table_hbm, inverse_ref, out_ref,
    order_ref, boundary_ref, table_ref,
    legendre, table, inverse, got, keep, send, landed, stage, solved,
    load_sem, first_send, first_recv, second_send, second_recv, out_sem,
):
    slots, degrees, latitudes = legendre.shape
    columns = grid_ref.shape[2]
    band = grid_ref.shape[1]
    devices = landed.shape[1]
    share = landed.shape[2]
    tile = GROUP * share
    width = stage.shape[2]
    orders = stage.shape[1] // share
    ma = lax.axis_index("ma")
    row = lax.axis_index("row")
    me = ma * rows + row
    z = me // GROUP
    w = me % GROUP
    z_order = (GROUPS - 1 - z, (z + GROUPS // 2) % GROUPS, z + 1 - 2 * (z % 2), z)
    inner = z * (GROUPS - 1 - z) // 2
    outer = 1 - inner
    turns = tuple(
        z_order[place] + inner * (z_order[(place + 2) % 4] - z_order[place]) for place in range(4)
    )
    skips = (0, inner, 0, outer)

    loads = [
        pltpu.make_async_copy(legendre_ref, legendre, load_sem.at[0]),
        pltpu.make_async_copy(table_hbm, table_ref, load_sem.at[1]),
        pltpu.make_async_copy(inverse_ref, inverse, load_sem.at[2]),
        pltpu.make_async_copy(order_hbm, order_ref, load_sem.at[3]),
        pltpu.make_async_copy(boundary_hbm, boundary_ref, load_sem.at[4]),
    ]
    for load in loads:
        load.start()

    barrier = pltpu.get_barrier_semaphore()

    @pl.loop(1, devices)
    def _(k):
        other = (me + k) % devices
        pl.semaphore_signal(
            barrier, inc=1, device_id=(other // rows, other % rows), device_id_type=MESH
        )

    pl.semaphore_wait(barrier, devices - 1)

    def to_slots(slot):
        here = got.at[slot, row, pl.ds(pl.multiple_of(ma * band, 16), band)]

        def send_to(other):
            pltpu.make_async_remote_copy(
                src_ref=grid_ref.at[other * slots + slot],
                dst_ref=here,
                send_sem=first_send.at[slot],
                recv_sem=first_recv.at[slot],
                device_id=(other // rows, other % rows),
                device_id_type=MESH,
            ).start()

        for pair in range(0, 4, 2):
            @pl.loop(1, GROUP)
            def _(k, pair=pair):
                for there in turns[pair:pair + 2]:
                    send_to(there * GROUP + (w + k) % GROUP)

            send_to(turns[pair] * GROUP + w)

            @pl.loop(skips[pair + 1], 1)
            def _(k, pair=pair):
                send_to(turns[pair + 1] * GROUP + w)

        pltpu.make_async_copy(
            grid_ref.at[me * slots + slot], here, first_recv.at[slot]
        ).start()

    for slot in range(slots):
        to_slots(slot)

    for load in loads[1:]:
        load.wait()
    full = table_ref[...]
    table[0] = full.astype(jnp.bfloat16)
    table[1] = (full - table[0].astype(jnp.float32)).astype(jnp.bfloat16)
    column = lax.broadcasted_iota(jnp.int32, keep.shape, 1)
    mode = column % width
    field = (column // width) % 2
    first = jnp.where(field == 0, boundary_ref[0, 0], boundary_ref[1, 0])
    last = jnp.where(field == 0, boundary_ref[0, 1], boundary_ref[1, 1])
    keep[...] = jnp.where((mode == first) | (mode == last), 0.0, 1.0)

    def analyse(slot, there):
        start = pl.multiple_of(there * tile, tile)
        grid = jnp.concatenate([got[slot, band_row] for band_row in range(rows)], axis=1)
        spectrum = jnp.dot(
            legendre[slot, pl.ds(start, tile), :], grid, preferred_element_type=jnp.float32
        )
        degree = start + lax.broadcasted_iota(jnp.int32, spectrum.shape, 0)
        spectrum = jnp.where(degree >= order_ref[slot], spectrum, 0.0)
        high = spectrum.astype(jnp.bfloat16)
        low = (spectrum - high.astype(jnp.float32)).astype(jnp.bfloat16)
        right = jnp.dot(high, table[0], preferred_element_type=jnp.float32)
        right += jnp.dot(low, table[0], preferred_element_type=jnp.float32)
        right += jnp.dot(high, table[1], preferred_element_type=jnp.float32)
        right = jnp.where(keep[0:1, :] > 0.0, right, 0.0)
        send[slot, pl.ds(start, tile), :] = right.astype(jnp.bfloat16)

    def piece(slot, other, at, count):
        return send.at[slot, pl.ds(pl.multiple_of(other * share + at, 16), count)]

    def to_degree(slot, other, half):
        at, count = (0, share) if half is None else (half * (share // 2), share // 2)
        sem = second_recv.at[slot, half or 0, z]
        here = landed.at[slot, me, pl.ds(at, count)]
        return piece(slot, other, at, count), here, sem

    def copy_to(slot, other, half=None):
        source, here, sem = to_degree(slot, other, half)
        pltpu.make_async_remote_copy(
            src_ref=source,
            dst_ref=here,
            send_sem=second_send.at[slot],
            recv_sem=sem,
            device_id=(other // rows, other % rows),
            device_id_type=MESH,
        ).start()

    def keep_own(slot, half=None):
        source, here, sem = to_degree(slot, me, half)
        pltpu.make_async_copy(source, here, sem).start()

    def wait_bytes(ref, sem):
        pltpu.make_async_copy(ref, ref, sem).wait()

    loads[0].wait()
    upper = z >= GROUPS // 2
    wait_bytes(got.at[0], first_recv.at[0])
    for there, skip in zip(turns, skips):
        analyse(0, there)

        @pl.loop(skip, GROUP)
        def _(k, there=there):
            copy_to(0, there * GROUP + (w + k) % GROUP)

    keep_own(0)
    wait_bytes(got.at[1], first_recv.at[1])
    up = z // (GROUPS // 2)
    one = GROUPS - 1 + up * (z_order[2] - (GROUPS - 1))
    two = GROUPS - 2 + up * (z - (GROUPS - 2))

    def copy_half(there, skip, half):
        @pl.loop(skip, GROUP)
        def _(k):
            copy_to(1, there * GROUP + (w + k) % GROUP, half)

    analyse(1, one)
    copy_half(one, 0, 0)
    analyse(1, two)
    copy_half(two, up, 0)
    copy_half(one, 0, 1)
    copy_half(two, up, 1)

    @pl.when(upper)
    def _():
        keep_own(1, 0)
        keep_own(1, 1)

    def put(slot, source, at, value):
        for part in range(2):
            for q in range(2):
                first_row = at * orders + source * 2 * slots + 2 * slot + part
                column = (2 * part + q) * width
                stage[q, pl.ds(first_row, value.shape[0], stride=orders), :] = value[
                    :, column:column + width
                ]

    def gather(slot, half=None):
        at, count = (0, share) if half is None else (half * (share // 2), share // 2)
        for source_z in z_order[::-1]:
            part = landed.at[slot, pl.ds(source_z * GROUP, GROUP), pl.ds(at, count)]
            wait_bytes(part, second_recv.at[slot, half or 0, source_z])

            @pl.loop(0, GROUP)
            def _(k):
                source = source_z * GROUP + k
                put(slot, source, at, landed[slot, source, at:at + count].astype(jnp.float32))

    @pl.when(jnp.logical_not(upper))
    def _():
        @pl.loop(0, devices)
        def _(source):
            put(1, source, 0, jnp.zeros((share, 4 * width), jnp.float32))

    gather(0)
    some = share // 4
    for step in range(4):
        if step % 2 == 0:
            @pl.when(upper)
            def _(step=step):
                gather(1, step // 2)

        @pl.loop(0, some, unroll=4)
        def _(k, step=step):
            l = step * some + k
            at = pl.ds(pl.multiple_of(l * orders, orders), orders)
            right = jnp.concatenate([stage[0, at, :], stage[1, at, :]], axis=1)
            solved[l] = lax.dot_general(
                inverse[l], right.astype(jnp.bfloat16), (((1,), (1,)), ((), ())),
                preferred_element_type=jnp.float32,
            ).astype(jnp.bfloat16)

        done = pl.ds(step * some, some)
        pltpu.make_async_copy(solved.at[done], out_ref.at[done], out_sem).start()

    for slot in range(slots):
        wait_bytes(grid_ref.at[pl.ds(0, devices - 1)], first_send.at[slot])
    wait_bytes(send.at[0, pl.ds(0, (devices - 1) * share)], second_send.at[0])

    @pl.when(upper)
    def _():
        wait_bytes(send.at[1, pl.ds(0, (devices // 2 - 1) * share)], second_send.at[1])

    @pl.when(jnp.logical_not(upper))
    def _():
        wait_bytes(send.at[1, pl.ds(0, devices // 2 * share)], second_send.at[1])

    wait_bytes(solved, out_sem)


def on_device(grid_field, legendre, order_table, boundary_rows, inverse):
    rows = lax.axis_size("row")
    devices = lax.axis_size("ma") * rows
    slots, degrees, latitudes = legendre.shape
    band, columns = grid_field.shape[1:]
    share = degrees // devices
    full_width = columns * rows
    orders = 2 * slots * devices
    fits = (
        devices == GROUP * GROUPS and slots == 2 and share % 32 == 0 and band % 16 == 0
        and columns % 128 == 0 and full_width == 512
    )
    if not fits:
        return with_collectives(grid_field, legendre, order_table, boundary_rows, inverse)
    width = full_width // 4
    any_space = pl.BlockSpec(memory_space=pl.ANY)
    dma = pltpu.SemaphoreType.DMA
    operands = (
        order_table, boundary_rows, grid_field, legendre, jnp.asarray(radial_parts(width)), inverse
    )
    operands = [pltpu.with_memory_space_constraint(each, pltpu.HBM) for each in operands]
    return pl.pallas_call(
        functools.partial(kernel, rows),
        out_shape=jax.ShapeDtypeStruct((share, 2 * width, orders), jnp.bfloat16),
        in_specs=[pl.BlockSpec(memory_space=pltpu.HBM)] * 6,
        out_specs=any_space,
        scratch_shapes=[
            pltpu.SMEM(order_table.shape, jnp.int32),
            pltpu.SMEM(boundary_rows.shape, jnp.int32),
            pltpu.VMEM((full_width, full_width), jnp.float32),
            pltpu.VMEM(legendre.shape, jnp.bfloat16),
            pltpu.VMEM((2, full_width, full_width), jnp.bfloat16),
            pltpu.VMEM(inverse.shape, jnp.bfloat16),
            pltpu.VMEM((slots, rows, latitudes, columns), jnp.bfloat16),
            pltpu.VMEM((8, full_width), jnp.float32),
            pltpu.VMEM((slots, degrees, full_width), jnp.bfloat16),
            pltpu.VMEM((slots, devices, share, full_width), jnp.bfloat16),
            pltpu.VMEM((2, share * orders, width), jnp.float32),
            pltpu.VMEM((share, 2 * width, orders), jnp.bfloat16),
            dma((5,)), dma((slots,)), dma((slots,)), dma((slots,)), dma((slots, 2, GROUPS)), dma,
        ],
        compiler_params=pltpu.CompilerParams(
            collective_id=0, has_side_effects=True, vmem_limit_bytes=44 * 2 ** 20
        ),
        cost_estimate=pl.CostEstimate(
            flops=6 * 10 ** 9, bytes_accessed=18 * 2 ** 20, transcendentals=0
        ),
    )(*operands)


def solution(mesh):
    return jax.shard_map(
        on_device,
        mesh=mesh,
        in_specs=(
            P(None, "ma", "row"),
            P(("ma", "row"), None, None),
            P(("ma", "row")),
            P(),
            P(("ma", "row"), None, None),
        ),
        out_specs=P(("ma", "row"), None, None),
        check_vma=False,
    )
```

```python
import functools

import jax
import jax.numpy as jnp
import numpy as np
from jax import lax
from jax.experimental import pallas as pl
from jax.experimental.pallas import tpu as pltpu
from jax.sharding import PartitionSpec as P

MESH = pl.DeviceIdType.MESH
GROUP = 8
GROUPS = 4


def chebyshev_table(radial_levels):
    wave_number = jnp.arange(radial_levels, dtype=jnp.float32)[:, None]
    grid_point = jnp.arange(radial_levels, dtype=jnp.float32)[None, :]
    cos_table = jnp.cos(jnp.pi * wave_number * (grid_point + 0.5) / radial_levels) * jnp.sqrt(
        2.0 / radial_levels
    )
    return jnp.where(wave_number == 0.0, cos_table * jnp.sqrt(0.5), cos_table)


def boundary_keep(boundary_rows, radial_levels):
    row_index = jnp.arange(radial_levels, dtype=jnp.int32)[None, :]
    boundary_hit = (row_index == boundary_rows[:, 0:1]) | (row_index == boundary_rows[:, 1:2])
    return jnp.where(boundary_hit, 0.0, 1.0).astype(jnp.float32)


def radial_matrix(boundary_rows, radial_levels):
    cheb = chebyshev_table(radial_levels)
    keep = boundary_keep(boundary_rows, radial_levels)
    eye = jnp.eye(2, dtype=jnp.float32)
    full = (
        cheb.T[:, None, None, None, None, :]
        * eye[None, :, None, None, :, None]
        * eye[None, None, :, :, None, None]
        * keep[None, None, None, None, :, :]
    )
    return full.reshape(4 * radial_levels, 4 * radial_levels)


def with_collectives(grid_field, legendre, order_table, boundary_rows, inverse):
    ma_count = lax.axis_size("ma")
    row_count = lax.axis_size("row")
    devices = ma_count * row_count
    slots, degree_total, latitudes = legendre.shape
    columns = grid_field.shape[2]
    radial_levels = columns * row_count // 4
    share = degree_total // devices
    got = lax.all_to_all(
        grid_field.reshape(devices, slots, latitudes // ma_count, columns),
        ("ma", "row"), split_axis=0, concat_axis=0, tiled=True,
    )
    got = got.reshape(ma_count, row_count, slots, latitudes // ma_count, columns)
    got = got.transpose(2, 0, 3, 1, 4).reshape(slots, latitudes, row_count * columns)
    spectrum = jnp.einsum("xlt,xtd->xld", legendre, got, preferred_element_type=jnp.float32)
    degrees = jnp.arange(degree_total, dtype=jnp.int32)
    lower = degrees[None, :] >= order_table[:, None]
    spectrum = jnp.where(lower[:, :, None], spectrum, 0.0)
    matrix = radial_matrix(boundary_rows, radial_levels)
    matrix_high = matrix.astype(jnp.bfloat16)
    matrix_low = (matrix - matrix_high.astype(jnp.float32)).astype(jnp.bfloat16)
    high = spectrum.astype(jnp.bfloat16)
    low = (spectrum - high.astype(jnp.float32)).astype(jnp.bfloat16)

    def mul(a, b):
        return jnp.einsum("xld,de->xle", a, b, preferred_element_type=jnp.float32)

    right = mul(high, matrix_high) + (mul(low, matrix_high) + mul(high, matrix_low))
    right = right.astype(jnp.bfloat16).reshape(slots, degree_total, 2, 2 * radial_levels)
    right = right.transpose(1, 0, 2, 3).reshape(devices, share, 2 * slots, 2 * radial_levels)
    right = lax.all_to_all(right, ("ma", "row"), split_axis=0, concat_axis=0, tiled=True)
    right = right.transpose(1, 0, 2, 3).reshape(share, devices * 2 * slots, 2 * radial_levels)
    solved = jnp.einsum("lij,lnj->lin", inverse, right, preferred_element_type=jnp.float32)
    return solved.astype(jnp.bfloat16)


def radial_parts(radial_levels):
    wave_number = np.arange(radial_levels, dtype=np.float64)[:, None]
    point = np.arange(radial_levels, dtype=np.float64)[None, :] + 0.5
    cheb = np.cos(np.pi * wave_number * point / radial_levels) * np.sqrt(2.0 / radial_levels)
    cheb[0] *= np.sqrt(0.5)
    full = np.zeros((radial_levels, 2, 2, 2, 2, radial_levels), np.float32)
    for q in range(2):
        for p in range(2):
            full[:, q, p, p, q, :] = cheb.T
    full = full.reshape(4 * radial_levels, 4 * radial_levels)
    return full


def kernel(
    rows, order_hbm, boundary_hbm, grid_ref, legendre_ref, table_hbm, inverse_ref, out_ref,
    order_ref, boundary_ref, table_ref,
    legendre, table, inverse, got, keep, send, landed, stage, solved,
    load_sem, first_send, first_recv, second_send, second_recv, out_sem,
):
    slots, degrees, latitudes = legendre.shape
    columns = grid_ref.shape[2]
    band = grid_ref.shape[1]
    devices = landed.shape[1]
    share = landed.shape[2]
    tile = GROUP * share
    width = stage.shape[2]
    orders = stage.shape[1] // share
    ma = lax.axis_index("ma")
    row = lax.axis_index("row")
    me = ma * rows + row
    z = me // GROUP
    w = me % GROUP
    z_order = (GROUPS - 1 - z, (z + GROUPS // 2) % GROUPS, z + 1 - 2 * (z % 2), z)
    inner = z * (GROUPS - 1 - z) // 2
    outer = 1 - inner
    turns = tuple(
        z_order[place] + inner * (z_order[(place + 2) % 4] - z_order[place]) for place in range(4)
    )
    skips = (0, inner, 0, outer)

    loads = [
        pltpu.make_async_copy(legendre_ref, legendre, load_sem.at[0]),
        pltpu.make_async_copy(table_hbm, table_ref, load_sem.at[1]),
        pltpu.make_async_copy(inverse_ref, inverse, load_sem.at[2]),
        pltpu.make_async_copy(order_hbm, order_ref, load_sem.at[3]),
        pltpu.make_async_copy(boundary_hbm, boundary_ref, load_sem.at[4]),
    ]
    for load in loads:
        load.start()

    barrier = pltpu.get_barrier_semaphore()

    @pl.loop(1, devices)
    def _(k):
        other = (me + k) % devices
        pl.semaphore_signal(
            barrier, inc=1, device_id=(other // rows, other % rows), device_id_type=MESH
        )

    pl.semaphore_wait(barrier, devices - 1)

    def to_slots(slot, pair):
        here = got.at[slot, row, pl.ds(pl.multiple_of(ma * band, 16), band)]

        def send_to(other):
            pltpu.make_async_remote_copy(
                src_ref=grid_ref.at[other * slots + slot],
                dst_ref=here,
                send_sem=first_send.at[slot, pair],
                recv_sem=first_recv.at[slot],
                device_id=(other // rows, other % rows),
                device_id_type=MESH,
            ).start()

        one, two = turns[2 * pair:2 * pair + 2]

        @pl.loop(1, GROUP)
        def _(k):
            send_to(one * GROUP + (w + k) % GROUP)
            send_to(two * GROUP + (w + k) % GROUP)

        send_to(one * GROUP + w)

        @pl.loop(skips[2 * pair + 1], 1)
        def _(k):
            send_to(two * GROUP + w)

        if pair == 1:
            pltpu.make_async_copy(
                grid_ref.at[me * slots + slot], here, first_recv.at[slot]
            ).start()

    def wait_bytes(ref, sem):
        pltpu.make_async_copy(ref, ref, sem).wait()

    def left(slot, pair):
        own = skips[2 * pair + 1]
        for less in range(2):
            @pl.when(own == less)
            def _(less=less):
                wait_bytes(
                    grid_ref.at[pl.ds(0, 2 * GROUP - less)], first_send.at[slot, pair]
                )

    to_slots(0, 0)
    to_slots(0, 1)

    for load in loads[1:]:
        load.wait()
    full = table_ref[...]
    table[0] = full.astype(jnp.bfloat16)
    table[1] = (full - table[0].astype(jnp.float32)).astype(jnp.bfloat16)
    column = lax.broadcasted_iota(jnp.int32, keep.shape, 1)
    mode = column % width
    field = (column // width) % 2
    first = jnp.where(field == 0, boundary_ref[0, 0], boundary_ref[1, 0])
    last = jnp.where(field == 0, boundary_ref[0, 1], boundary_ref[1, 1])
    keep[...] = jnp.where((mode == first) | (mode == last), 0.0, 1.0)

    def analyse(slot, there):
        start = pl.multiple_of(there * tile, tile)
        grid = jnp.concatenate([got[slot, band_row] for band_row in range(rows)], axis=1)
        spectrum = jnp.dot(
            legendre[slot, pl.ds(start, tile), :], grid, preferred_element_type=jnp.float32
        )
        degree = start + lax.broadcasted_iota(jnp.int32, spectrum.shape, 0)
        spectrum = jnp.where(degree >= order_ref[slot], spectrum, 0.0)
        high = spectrum.astype(jnp.bfloat16)
        low = (spectrum - high.astype(jnp.float32)).astype(jnp.bfloat16)
        right = jnp.dot(high, table[0], preferred_element_type=jnp.float32)
        right += jnp.dot(low, table[0], preferred_element_type=jnp.float32)
        right += jnp.dot(high, table[1], preferred_element_type=jnp.float32)
        right = jnp.where(keep[0:1, :] > 0.0, right, 0.0)
        send[slot, pl.ds(start, tile), :] = right.astype(jnp.bfloat16)

    def piece(slot, other, at, count):
        return send.at[slot, pl.ds(pl.multiple_of(other * share + at, 16), count)]

    def to_degree(slot, other, half):
        at, count = (0, share) if half is None else (half * (share // 2), share // 2)
        sem = second_recv.at[slot, half or 0, z]
        here = landed.at[slot, me, pl.ds(at, count)]
        return piece(slot, other, at, count), here, sem

    def copy_to(slot, other, half=None):
        source, here, sem = to_degree(slot, other, half)
        pltpu.make_async_remote_copy(
            src_ref=source,
            dst_ref=here,
            send_sem=second_send.at[slot],
            recv_sem=sem,
            device_id=(other // rows, other % rows),
            device_id_type=MESH,
        ).start()

    def keep_own(slot, half=None):
        source, here, sem = to_degree(slot, me, half)
        pltpu.make_async_copy(source, here, sem).start()

    for pair in range(2):
        left(0, pair)
        to_slots(1, pair)

    loads[0].wait()
    upper = z >= GROUPS // 2
    wait_bytes(got.at[0], first_recv.at[0])
    for there in turns:
        analyse(0, there)
    wait_bytes(got.at[1], first_recv.at[1])
    for there, skip in zip(turns, skips):
        @pl.loop(skip, GROUP)
        def _(k, there=there):
            copy_to(0, there * GROUP + (w + k) % GROUP)

    keep_own(0)
    up = z // (GROUPS // 2)
    one = GROUPS - 1 + up * (z_order[2] - (GROUPS - 1))
    two = GROUPS - 2 + up * (z - (GROUPS - 2))

    def copy_half(there, skip, half):
        @pl.loop(skip, GROUP)
        def _(k):
            copy_to(1, there * GROUP + (w + k) % GROUP, half)

    analyse(1, one)
    copy_half(one, 0, 0)
    analyse(1, two)
    copy_half(two, up, 0)
    copy_half(one, 0, 1)
    copy_half(two, up, 1)

    @pl.when(upper)
    def _():
        keep_own(1, 0)
        keep_own(1, 1)

    def put(slot, source, at, value):
        for part in range(2):
            for q in range(2):
                first_row = at * orders + source * 2 * slots + 2 * slot + part
                column = (2 * part + q) * width
                stage[q, pl.ds(first_row, value.shape[0], stride=orders), :] = value[
                    :, column:column + width
                ]

    def gather(slot, half=None):
        at, count = (0, share) if half is None else (half * (share // 2), share // 2)
        for source_z in z_order[::-1]:
            part = landed.at[slot, pl.ds(source_z * GROUP, GROUP), pl.ds(at, count)]
            wait_bytes(part, second_recv.at[slot, half or 0, source_z])

            @pl.loop(0, GROUP)
            def _(k):
                source = source_z * GROUP + k
                put(slot, source, at, landed[slot, source, at:at + count].astype(jnp.float32))

    @pl.when(jnp.logical_not(upper))
    def _():
        @pl.loop(0, devices)
        def _(source):
            put(1, source, 0, jnp.zeros((share, 4 * width), jnp.float32))

    gather(0)
    some = share // 4
    for step in range(4):
        if step % 2 == 0:
            @pl.when(upper)
            def _(step=step):
                gather(1, step // 2)

        @pl.loop(0, some, unroll=4)
        def _(k, step=step):
            l = step * some + k
            at = pl.ds(pl.multiple_of(l * orders, orders), orders)
            right = jnp.concatenate([stage[0, at, :], stage[1, at, :]], axis=1)
            solved[l] = lax.dot_general(
                inverse[l], right.astype(jnp.bfloat16), (((1,), (1,)), ((), ())),
                preferred_element_type=jnp.float32,
            ).astype(jnp.bfloat16)

        done = pl.ds(step * some, some)
        pltpu.make_async_copy(solved.at[done], out_ref.at[done], out_sem).start()

    for pair in range(2):
        left(1, pair)
    wait_bytes(send.at[0, pl.ds(0, (devices - 1) * share)], second_send.at[0])

    @pl.when(upper)
    def _():
        wait_bytes(send.at[1, pl.ds(0, (devices // 2 - 1) * share)], second_send.at[1])

    @pl.when(jnp.logical_not(upper))
    def _():
        wait_bytes(send.at[1, pl.ds(0, devices // 2 * share)], second_send.at[1])

    wait_bytes(solved, out_sem)


def on_device(grid_field, legendre, order_table, boundary_rows, inverse):
    rows = lax.axis_size("row")
    devices = lax.axis_size("ma") * rows
    slots, degrees, latitudes = legendre.shape
    band, columns = grid_field.shape[1:]
    share = degrees // devices
    full_width = columns * rows
    orders = 2 * slots * devices
    fits = (
        devices == GROUP * GROUPS and slots == 2 and share % 32 == 0 and band % 16 == 0
        and columns % 128 == 0 and full_width == 512
    )
    if not fits:
        return with_collectives(grid_field, legendre, order_table, boundary_rows, inverse)
    width = full_width // 4
    any_space = pl.BlockSpec(memory_space=pl.ANY)
    dma = pltpu.SemaphoreType.DMA
    operands = (
        order_table, boundary_rows, grid_field, legendre, jnp.asarray(radial_parts(width)), inverse
    )
    operands = [pltpu.with_memory_space_constraint(each, pltpu.HBM) for each in operands]
    return pl.pallas_call(
        functools.partial(kernel, rows),
        out_shape=jax.ShapeDtypeStruct((share, 2 * width, orders), jnp.bfloat16),
        in_specs=[pl.BlockSpec(memory_space=pltpu.HBM)] * 6,
        out_specs=any_space,
        scratch_shapes=[
            pltpu.SMEM(order_table.shape, jnp.int32),
            pltpu.SMEM(boundary_rows.shape, jnp.int32),
            pltpu.VMEM((full_width, full_width), jnp.float32),
            pltpu.VMEM(legendre.shape, jnp.bfloat16),
            pltpu.VMEM((2, full_width, full_width), jnp.bfloat16),
            pltpu.VMEM(inverse.shape, jnp.bfloat16),
            pltpu.VMEM((slots, rows, latitudes, columns), jnp.bfloat16),
            pltpu.VMEM((8, full_width), jnp.float32),
            pltpu.VMEM((slots, degrees, full_width), jnp.bfloat16),
            pltpu.VMEM((slots, devices, share, full_width), jnp.bfloat16),
            pltpu.VMEM((2, share * orders, width), jnp.float32),
            pltpu.VMEM((share, 2 * width, orders), jnp.bfloat16),
            dma((5,)), dma((slots, 2)), dma((slots,)), dma((slots,)), dma((slots, 2, GROUPS)), dma,
        ],
        compiler_params=pltpu.CompilerParams(
            collective_id=0, has_side_effects=True, vmem_limit_bytes=44 * 2 ** 20
        ),
        cost_estimate=pl.CostEstimate(
            flops=6 * 10 ** 9, bytes_accessed=18 * 2 ** 20, transcendentals=0
        ),
    )(*operands)


def solution(mesh):
    return jax.shard_map(
        on_device,
        mesh=mesh,
        in_specs=(
            P(None, "ma", "row"),
            P(("ma", "row"), None, None),
            P(("ma", "row")),
            P(),
            P(("ma", "row"), None, None),
        ),
        out_specs=P(("ma", "row"), None, None),
        check_vma=False,
    )
```

```python
import functools

import jax
import jax.numpy as jnp
import numpy as np
from jax import lax
from jax.experimental import pallas as pl
from jax.experimental.pallas import tpu as pltpu
from jax.sharding import PartitionSpec as P

MESH = pl.DeviceIdType.MESH
GROUP = 8
GROUPS = 4


def chebyshev_table(radial_levels):
    wave_number = jnp.arange(radial_levels, dtype=jnp.float32)[:, None]
    grid_point = jnp.arange(radial_levels, dtype=jnp.float32)[None, :]
    cos_table = jnp.cos(jnp.pi * wave_number * (grid_point + 0.5) / radial_levels) * jnp.sqrt(
        2.0 / radial_levels
    )
    return jnp.where(wave_number == 0.0, cos_table * jnp.sqrt(0.5), cos_table)


def boundary_keep(boundary_rows, radial_levels):
    row_index = jnp.arange(radial_levels, dtype=jnp.int32)[None, :]
    boundary_hit = (row_index == boundary_rows[:, 0:1]) | (row_index == boundary_rows[:, 1:2])
    return jnp.where(boundary_hit, 0.0, 1.0).astype(jnp.float32)


def radial_matrix(boundary_rows, radial_levels):
    cheb = chebyshev_table(radial_levels)
    keep = boundary_keep(boundary_rows, radial_levels)
    eye = jnp.eye(2, dtype=jnp.float32)
    full = (
        cheb.T[:, None, None, None, None, :]
        * eye[None, :, None, None, :, None]
        * eye[None, None, :, :, None, None]
        * keep[None, None, None, None, :, :]
    )
    return full.reshape(4 * radial_levels, 4 * radial_levels)


def with_collectives(grid_field, legendre, order_table, boundary_rows, inverse):
    ma_count = lax.axis_size("ma")
    row_count = lax.axis_size("row")
    devices = ma_count * row_count
    slots, degree_total, latitudes = legendre.shape
    columns = grid_field.shape[2]
    radial_levels = columns * row_count // 4
    share = degree_total // devices
    got = lax.all_to_all(
        grid_field.reshape(devices, slots, latitudes // ma_count, columns),
        ("ma", "row"), split_axis=0, concat_axis=0, tiled=True,
    )
    got = got.reshape(ma_count, row_count, slots, latitudes // ma_count, columns)
    got = got.transpose(2, 0, 3, 1, 4).reshape(slots, latitudes, row_count * columns)
    spectrum = jnp.einsum("xlt,xtd->xld", legendre, got, preferred_element_type=jnp.float32)
    degrees = jnp.arange(degree_total, dtype=jnp.int32)
    lower = degrees[None, :] >= order_table[:, None]
    spectrum = jnp.where(lower[:, :, None], spectrum, 0.0)
    matrix = radial_matrix(boundary_rows, radial_levels)
    matrix_high = matrix.astype(jnp.bfloat16)
    matrix_low = (matrix - matrix_high.astype(jnp.float32)).astype(jnp.bfloat16)
    high = spectrum.astype(jnp.bfloat16)
    low = (spectrum - high.astype(jnp.float32)).astype(jnp.bfloat16)

    def mul(a, b):
        return jnp.einsum("xld,de->xle", a, b, preferred_element_type=jnp.float32)

    right = mul(high, matrix_high) + (mul(low, matrix_high) + mul(high, matrix_low))
    right = right.astype(jnp.bfloat16).reshape(slots, degree_total, 2, 2 * radial_levels)
    right = right.transpose(1, 0, 2, 3).reshape(devices, share, 2 * slots, 2 * radial_levels)
    right = lax.all_to_all(right, ("ma", "row"), split_axis=0, concat_axis=0, tiled=True)
    right = right.transpose(1, 0, 2, 3).reshape(share, devices * 2 * slots, 2 * radial_levels)
    solved = jnp.einsum("lij,lnj->lin", inverse, right, preferred_element_type=jnp.float32)
    return solved.astype(jnp.bfloat16)


def radial_parts(radial_levels):
    wave_number = np.arange(radial_levels, dtype=np.float64)[:, None]
    point = np.arange(radial_levels, dtype=np.float64)[None, :] + 0.5
    cheb = np.cos(np.pi * wave_number * point / radial_levels) * np.sqrt(2.0 / radial_levels)
    cheb[0] *= np.sqrt(0.5)
    full = np.zeros((radial_levels, 2, 2, 2, 2, radial_levels), np.float32)
    for q in range(2):
        for p in range(2):
            full[:, q, p, p, q, :] = cheb.T
    full = full.reshape(4 * radial_levels, 4 * radial_levels)
    return full


def kernel(
    rows, order_hbm, boundary_hbm, grid_ref, legendre_ref, table_hbm, inverse_ref, out_ref,
    order_ref, boundary_ref, table_ref,
    legendre, table, inverse, got, keep, send, landed, stage, solved,
    load_sem, first_send, first_recv, second_send, second_recv, out_sem,
):
    slots, degrees, latitudes = legendre.shape
    columns = grid_ref.shape[2]
    band = grid_ref.shape[1]
    devices = landed.shape[1]
    share = landed.shape[2]
    tile = GROUP * share
    width = stage.shape[2]
    orders = 2 * slots * devices
    ma = lax.axis_index("ma")
    row = lax.axis_index("row")
    me = ma * rows + row
    z = me // GROUP
    w = me % GROUP
    z_order = (GROUPS - 1 - z, (z + GROUPS // 2) % GROUPS, z + 1 - 2 * (z % 2), z)
    inner = z * (GROUPS - 1 - z) // 2
    outer = 1 - inner
    turns = tuple(
        z_order[place] + inner * (z_order[(place + 2) % 4] - z_order[place]) for place in range(4)
    )
    skips = (0, inner, 0, outer)

    loads = [
        pltpu.make_async_copy(legendre_ref, legendre, load_sem.at[0]),
        pltpu.make_async_copy(table_hbm, table_ref, load_sem.at[1]),
        pltpu.make_async_copy(inverse_ref, inverse, load_sem.at[2]),
        pltpu.make_async_copy(order_hbm, order_ref, load_sem.at[3]),
        pltpu.make_async_copy(boundary_hbm, boundary_ref, load_sem.at[4]),
    ]
    for load in loads:
        load.start()

    barrier = pltpu.get_barrier_semaphore()

    @pl.loop(1, devices)
    def _(k):
        other = (me + k) % devices
        pl.semaphore_signal(
            barrier, inc=1, device_id=(other // rows, other % rows), device_id_type=MESH
        )

    pl.semaphore_wait(barrier, devices - 1)

    def to_slots(slot):
        here = got.at[slot, row, pl.ds(pl.multiple_of(ma * band, 16), band)]

        def send_to(other):
            pltpu.make_async_remote_copy(
                src_ref=grid_ref.at[other * slots + slot],
                dst_ref=here,
                send_sem=first_send.at[slot],
                recv_sem=first_recv.at[slot],
                device_id=(other // rows, other % rows),
                device_id_type=MESH,
            ).start()

        for pair in range(0, 4, 2):
            @pl.loop(1, GROUP)
            def _(k, pair=pair):
                for there in turns[pair:pair + 2]:
                    send_to(there * GROUP + (w + k) % GROUP)

            send_to(turns[pair] * GROUP + w)

            @pl.loop(skips[pair + 1], 1)
            def _(k, pair=pair):
                send_to(turns[pair + 1] * GROUP + w)

        pltpu.make_async_copy(
            grid_ref.at[me * slots + slot], here, first_recv.at[slot]
        ).start()

    for slot in range(slots):
        to_slots(slot)

    for load in loads[1:]:
        load.wait()
    full = table_ref[...]
    table[0] = full.astype(jnp.bfloat16)
    table[1] = (full - table[0].astype(jnp.float32)).astype(jnp.bfloat16)
    column = lax.broadcasted_iota(jnp.int32, keep.shape, 1)
    mode = column % width
    field = (column // width) % 2
    first = jnp.where(field == 0, boundary_ref[0, 0], boundary_ref[1, 0])
    last = jnp.where(field == 0, boundary_ref[0, 1], boundary_ref[1, 1])
    keep[...] = jnp.where((mode == first) | (mode == last), 0.0, 1.0)

    def analyse(slot, there):
        start = pl.multiple_of(there * tile, tile)
        grid = jnp.concatenate([got[slot, band_row] for band_row in range(rows)], axis=1)
        spectrum = jnp.dot(
            legendre[slot, pl.ds(start, tile), :], grid, preferred_element_type=jnp.float32
        )
        degree = start + lax.broadcasted_iota(jnp.int32, spectrum.shape, 0)
        spectrum = jnp.where(degree >= order_ref[slot], spectrum, 0.0)
        high = spectrum.astype(jnp.bfloat16)
        low = (spectrum - high.astype(jnp.float32)).astype(jnp.bfloat16)
        right = jnp.dot(high, table[0], preferred_element_type=jnp.float32)
        right += jnp.dot(low, table[0], preferred_element_type=jnp.float32)
        right += jnp.dot(high, table[1], preferred_element_type=jnp.float32)
        right = jnp.where(keep[0:1, :] > 0.0, right, 0.0)
        send[slot, pl.ds(start, tile), :] = right.astype(jnp.bfloat16)

    def piece(slot, other, at, count):
        return send.at[slot, pl.ds(pl.multiple_of(other * share + at, 16), count)]

    def to_degree(slot, other, half):
        at, count = (0, share) if half is None else (half * (share // 2), share // 2)
        sem = second_recv.at[slot, half or 0, z]
        here = landed.at[slot, me, pl.ds(at, count)]
        return piece(slot, other, at, count), here, sem

    def copy_to(slot, other, half=None):
        source, here, sem = to_degree(slot, other, half)
        pltpu.make_async_remote_copy(
            src_ref=source,
            dst_ref=here,
            send_sem=second_send.at[slot],
            recv_sem=sem,
            device_id=(other // rows, other % rows),
            device_id_type=MESH,
        ).start()

    def keep_own(slot, half=None):
        source, here, sem = to_degree(slot, me, half)
        pltpu.make_async_copy(source, here, sem).start()

    def wait_bytes(ref, sem):
        pltpu.make_async_copy(ref, ref, sem).wait()

    loads[0].wait()
    upper = z >= GROUPS // 2
    wait_bytes(got.at[0], first_recv.at[0])
    for there, skip in zip(turns, skips):
        analyse(0, there)

        @pl.loop(skip, GROUP)
        def _(k, there=there):
            copy_to(0, there * GROUP + (w + k) % GROUP)

    keep_own(0)
    wait_bytes(got.at[1], first_recv.at[1])
    up = z // (GROUPS // 2)
    one = GROUPS - 1 + up * (z_order[2] - (GROUPS - 1))
    two = GROUPS - 2 + up * (z - (GROUPS - 2))

    def copy_half(there, skip, half):
        @pl.loop(skip, GROUP)
        def _(k):
            copy_to(1, there * GROUP + (w + k) % GROUP, half)

    analyse(1, one)
    copy_half(one, 0, 0)
    analyse(1, two)
    copy_half(two, up, 0)
    copy_half(one, 0, 1)
    copy_half(two, up, 1)

    @pl.when(upper)
    def _():
        keep_own(1, 0)
        keep_own(1, 1)

    def put(slot, source, at, value):
        for part in range(2):
            for q in range(2):
                first_row = at * orders + source * 2 * slots + 2 * slot + part
                column = (2 * part + q) * width
                stage[q, pl.ds(first_row, value.shape[0], stride=orders), :] = value[
                    :, column:column + width
                ]

    def gather(slot, half=None):
        at, count = (0, share) if half is None else (half * (share // 2), share // 2)
        for source_z in z_order[::-1]:
            part = landed.at[slot, pl.ds(source_z * GROUP, GROUP), pl.ds(at, count)]
            wait_bytes(part, second_recv.at[slot, half or 0, source_z])

            @pl.loop(0, GROUP, unroll=2)
            def _(k):
                source = source_z * GROUP + k
                put(slot, source, at, landed[slot, source, at:at + count].astype(jnp.float32))

    @pl.when(jnp.logical_not(upper))
    def _():
        @pl.loop(0, devices)
        def _(source):
            put(1, source, 0, jnp.zeros((share, 4 * width), jnp.float32))

    gather(0)
    some = share // 4
    for step in range(4):
        if step % 2 == 0:
            @pl.when(upper)
            def _(step=step):
                gather(1, step // 2)

        @pl.loop(0, some, unroll=8)
        def _(k, step=step):
            l = step * some + k
            at = pl.ds(pl.multiple_of(l * orders, orders), orders)
            right = jnp.concatenate([stage[0, at, :], stage[1, at, :]], axis=1)
            solved[l] = lax.dot_general(
                inverse[l], right.astype(jnp.bfloat16), (((1,), (1,)), ((), ())),
                preferred_element_type=jnp.float32,
            ).astype(jnp.bfloat16)

        done = pl.ds(step * some, some)
        pltpu.make_async_copy(solved.at[done], out_ref.at[done], out_sem).start()

    for slot in range(slots):
        wait_bytes(grid_ref.at[pl.ds(0, devices - 1)], first_send.at[slot])
    wait_bytes(send.at[0, pl.ds(0, (devices - 1) * share)], second_send.at[0])

    @pl.when(upper)
    def _():
        wait_bytes(send.at[1, pl.ds(0, (devices // 2 - 1) * share)], second_send.at[1])

    @pl.when(jnp.logical_not(upper))
    def _():
        wait_bytes(send.at[1, pl.ds(0, devices // 2 * share)], second_send.at[1])

    wait_bytes(solved, out_sem)


def on_device(grid_field, legendre, order_table, boundary_rows, inverse):
    rows = lax.axis_size("row")
    devices = lax.axis_size("ma") * rows
    slots, degrees, latitudes = legendre.shape
    band, columns = grid_field.shape[1:]
    share = degrees // devices
    full_width = columns * rows
    orders = 2 * slots * devices
    fits = (
        devices == GROUP * GROUPS and slots == 2 and share % 32 == 0 and band % 16 == 0
        and columns % 128 == 0 and full_width == 512
    )
    if not fits:
        return with_collectives(grid_field, legendre, order_table, boundary_rows, inverse)
    width = full_width // 4
    any_space = pl.BlockSpec(memory_space=pl.ANY)
    dma = pltpu.SemaphoreType.DMA
    operands = (
        order_table, boundary_rows, grid_field, legendre, jnp.asarray(radial_parts(width)), inverse
    )
    operands = [pltpu.with_memory_space_constraint(each, pltpu.HBM) for each in operands]
    return pl.pallas_call(
        functools.partial(kernel, rows),
        out_shape=jax.ShapeDtypeStruct((share, 2 * width, orders), jnp.bfloat16),
        in_specs=[pl.BlockSpec(memory_space=pltpu.HBM)] * 6,
        out_specs=any_space,
        scratch_shapes=[
            pltpu.SMEM(order_table.shape, jnp.int32),
            pltpu.SMEM(boundary_rows.shape, jnp.int32),
            pltpu.VMEM((full_width, full_width), jnp.float32),
            pltpu.VMEM(legendre.shape, jnp.bfloat16),
            pltpu.VMEM((2, full_width, full_width), jnp.bfloat16),
            pltpu.VMEM(inverse.shape, jnp.bfloat16),
            pltpu.VMEM((slots, rows, latitudes, columns), jnp.bfloat16),
            pltpu.VMEM((8, full_width), jnp.float32),
            pltpu.VMEM((slots, degrees, full_width), jnp.bfloat16),
            pltpu.VMEM((slots, devices, share, full_width), jnp.bfloat16),
            pltpu.VMEM((2, (share + 1) * orders, width), jnp.float32),
            pltpu.VMEM((share, 2 * width, orders), jnp.bfloat16),
            dma((5,)), dma((slots,)), dma((slots,)), dma((slots,)), dma((slots, 2, GROUPS)), dma,
        ],
        compiler_params=pltpu.CompilerParams(
            collective_id=0, has_side_effects=True, vmem_limit_bytes=44 * 2 ** 20
        ),
        cost_estimate=pl.CostEstimate(
            flops=6 * 10 ** 9, bytes_accessed=18 * 2 ** 20, transcendentals=0
        ),
    )(*operands)


def solution(mesh):
    return jax.shard_map(
        on_device,
        mesh=mesh,
        in_specs=(
            P(None, "ma", "row"),
            P(("ma", "row"), None, None),
            P(("ma", "row")),
            P(),
            P(("ma", "row"), None, None),
        ),
        out_specs=P(("ma", "row"), None, None),
        check_vma=False,
    )
```
